256 devices in a mesh: kv: 8 (over z), roll: 32 (over x, y, core).
Axes of the slice: x: 4, y: 4, z: 8, core: 2. Of those that a mesh axis runs over, the one named last changes fastest.
Arguments:
- q_tokens: bfloat16 [1024, 24, 8192], P('roll', 'kv'), may hold values from -6 to 6
- grad_tokens: bfloat16 [1024, 24, 8192], P('roll', 'kv'), may hold values from -6 to 6
- roll_keys: bfloat16 [1024, 24, 1024], P('roll', 'kv'), may hold values from -6 to 6
- roll_values: bfloat16 [1024, 24, 1024], P('roll', 'kv'), may hold values from -6 to 6
- prompt_keys: bfloat16 [65536, 1024], P('roll', 'kv'), may hold values from -6 to 6
- prompt_values: bfloat16 [65536, 1024], P('roll', 'kv'), may hold values from -6 to 6
- slot_prompt: int32 [1024], replicated, may hold values from -1 to 31, as said below
- prompt_owner: int32 [32], replicated, may hold values from 0 to 31, each once
- roll_len: int32 [1024], replicated, may hold values from 1 to 24, as said below
- prompt_len: int32 [32], replicated, may hold values from 512 to 2048, as said below
Outputs:
- grad_query: bfloat16 [1024, 24, 8192], P('roll', 'kv')
- grad_roll_keys: bfloat16 [1024, 24, 1024], P('roll', 'kv')
- grad_roll_values: bfloat16 [1024, 24, 1024], P('roll', 'kv')
- grad_prompt_keys: bfloat16 [65536, 1024], P('roll', 'kv')
- grad_prompt_values: bfloat16 [65536, 1024], P('roll', 'kv')
The draws below stay inside these ranges and needn't reach their ends.
Inputs may be any that keep to these rules, and one draw needn't show every extreme that they name: `slot_prompt`: entry n names the prompt of the rollout in slot n, or -1 for an empty slot. Slots d * 32 to d * 32 + 31 belong to index d of roll, live slots first. Every prompt has exactly 16 rollouts; an index of roll holds 0 to 32 rollouts and at most 2 of one prompt; some index holds 32, and some index holds 2 of one prompt. `prompt_owner`: each index of roll holds exactly one prompt. `roll_len`: some slot has 24. `prompt_len`: some prompt has 2048.
All inputs are finite; a program needn't handle non-finite values.
Results may differ from the reference program's by a relative error of at most 0.008.
Values may be sent and summed in bfloat16 or wider, within the bound.
A program may use at most 128 MiB of HBM per device.

```python
import jax
import jax.numpy as jnp
from jax import lax

HD = 128
QH = 64
KVH = 8
HG = 8
GROUP = 16
RT = 24
PLEN = 2048
SLOTS = 32
TSLOTS = 1024
N_ROLL = 32


def draw_q_tokens(key, part):
    key = jax.random.fold_in(key, 11)
    key_base = jax.random.fold_in(key, 0)
    result = jax.random.truncated_normal(key_base, -6.0, 6.0, (TSLOTS, RT, QH * HD))
    return result.astype(jnp.bfloat16)


def draw_roll_keys(key, part):
    key = jax.random.fold_in(key, 23)
    result = jax.random.truncated_normal(key, -6.0, 6.0, (TSLOTS, RT, KVH * HD))
    return result.astype(jnp.bfloat16)


def draw_slot_prompt(key, part):
    key = jax.random.fold_in(key, 5)
    key_order, key_shift, key_names = jax.random.split(key, 3)
    ordering = jax.random.permutation(key_order, N_ROLL)
    shifts = 2 * jax.random.randint(key_shift, (N_ROLL // 2,), 0, GROUP // 2 + 1).astype(jnp.int32)
    shifts = shifts.at[0].set(GROUP)
    counts = jnp.zeros((N_ROLL,), jnp.int32)
    counts = counts.at[ordering[0::2]].set(GROUP + shifts).at[ordering[1::2]].set(GROUP - shifts)
    starts = jnp.cumsum(counts) - counts
    slot_ids = jnp.arange(SLOTS, dtype=jnp.int32)
    position = starts[:, None] + slot_ids[None, :]
    is_live = slot_ids[None, :] < counts[:, None]
    names = jax.random.permutation(key_names, N_ROLL).astype(jnp.int32)
    prompts = names[position // 2 % N_ROLL]
    return jnp.where(is_live, prompts, -1).reshape(-1).astype(jnp.int32)


def draw_roll_len(key, part):
    key = jax.random.fold_in(key, 7)
    lengths = jax.random.randint(key, (TSLOTS,), 1, RT + 1).astype(jnp.int32)
    return lengths.at[0].set(RT)


def draw_prompt_len(key, part):
    key = jax.random.fold_in(key, 9)
    lengths = jax.random.randint(key, (N_ROLL,), PLEN // 4, PLEN + 1).astype(jnp.int32)
    return lengths.at[0].set(PLEN)


def level_of(rng, dims, cuts, least, top_value):
    level = 1.0
    for dim, blocks in cuts:
        steps = jax.random.uniform(jax.random.fold_in(jax.random.fold_in(rng, 6), dim), (blocks,), jnp.float32, least / len(cuts), top_value / len(cuts))
        level = level * jnp.repeat(jnp.exp(steps), dims[dim] // blocks).reshape((-1,) + (1,) * (len(dims) - 1 - dim))
    return level


def normal_values(key, dims, width, limit, pieces=(), held_as=jnp.bfloat16):
    level = level_of(key, dims, pieces, -0.22, 0.18) if pieces else 1.0
    drawn = jax.random.normal(key, dims, jnp.float32) * width * level
    return jnp.minimum(jnp.maximum(drawn, -limit), limit).astype(held_as)


def setup_inputs(seed: int = 0) -> dict:
    splits = jax.random.split(jax.random.key(seed), 11)
    q_tokens = draw_q_tokens(jax.random.fold_in(splits[10], 71), 0)
    grad_tokens = normal_values(splits[1], (TSLOTS, RT, QH * HD), 1.0, 6.0, ((0, 32), (1, 8)))
    roll_keys = draw_roll_keys(jax.random.fold_in(splits[10], 71), 0)
    roll_values = normal_values(splits[3], (TSLOTS, RT, KVH * HD), 1.0, 6.0, ((0, 32), (1, 8)))
    prompt_keys = normal_values(splits[4], (N_ROLL * PLEN, KVH * HD), 1.0, 6.0, ((0, 32), (1, 8)))
    prompt_values = normal_values(splits[5], (N_ROLL * PLEN, KVH * HD), 1.0, 6.0, ((0, 32), (1, 8)))
    slot_prompt = draw_slot_prompt(jax.random.fold_in(splits[10], 71), 0)
    prompt_owner = jax.random.permutation(splits[7], N_ROLL).astype(jnp.int32)
    roll_len = draw_roll_len(jax.random.fold_in(splits[10], 71), 0)
    prompt_len = draw_prompt_len(jax.random.fold_in(splits[10], 71), 0)
    return dict(q_tokens=q_tokens, grad_tokens=grad_tokens, roll_keys=roll_keys, roll_values=roll_values, prompt_keys=prompt_keys, prompt_values=prompt_values, slot_prompt=slot_prompt, prompt_owner=prompt_owner, roll_len=roll_len, prompt_len=prompt_len)


def to_half(values):
    return lax.optimization_barrier(values.astype(jnp.bfloat16)).astype(jnp.float32)


def reference(q_tokens, grad_tokens, roll_keys, roll_values, prompt_keys, prompt_values, slot_prompt, prompt_owner, roll_len, prompt_len):
    softmax_scale = HD ** -0.5
    is_live = slot_prompt >= 0
    sort_key = jnp.where(is_live, slot_prompt, N_ROLL).astype(jnp.int32)
    ordering = jnp.argsort(sort_key, stable=True).astype(jnp.int32)
    members = ordering[: N_ROLL * GROUP].reshape(N_ROLL, GROUP)
    key_table = prompt_keys.reshape(N_ROLL, PLEN, KVH, HD)
    value_table = prompt_values.reshape(N_ROLL, PLEN, KVH, HD)
    tok_pos = jnp.arange(RT, dtype=jnp.int32)
    key_pos = jnp.arange(PLEN, dtype=jnp.int32)
    causal = (tok_pos[None, :] <= tok_pos[:, None])[None, :, None, None, :]

    def one_prompt(inputs):
        prompt, chosen = inputs
        holder = prompt_owner[prompt]
        pkeys = jnp.take(key_table, holder, axis=0).astype(jnp.float32)
        pvalues = jnp.take(value_table, holder, axis=0).astype(jnp.float32)
        visible = (key_pos < prompt_len[prompt])[None, None, None, None, :]
        lengths = jnp.take(roll_len, chosen)
        valid = tok_pos[None, :] < lengths[:, None]
        query = jnp.take(q_tokens, chosen, axis=0).astype(jnp.float32).reshape(GROUP, RT, KVH, HG, HD)
        grad_rows = jnp.take(grad_tokens, chosen, axis=0)
        grads = jnp.where(valid[:, :, None], grad_rows, jnp.zeros((), grad_rows.dtype)).astype(jnp.float32).reshape(GROUP, RT, KVH, HG, HD)
        own_keys = jnp.take(roll_keys, chosen, axis=0).astype(jnp.float32).reshape(GROUP, RT, KVH, HD)
        own_values = jnp.take(roll_values, chosen, axis=0).astype(jnp.float32).reshape(GROUP, RT, KVH, HD)
        prompt_scores = jnp.einsum("ntkjd,pkd->ntkjp", query, pkeys) * softmax_scale
        local_scores = jnp.einsum("ntkjd,nukd->ntkju", query, own_keys) * softmax_scale
        row_max = jnp.maximum(jnp.max(jnp.where(visible, prompt_scores, -jnp.inf), axis=-1),
                              jnp.max(jnp.where(causal, local_scores, -jnp.inf), axis=-1))
        prompt_exp = jnp.where(visible, jnp.exp(prompt_scores - row_max[..., None]), 0.0)
        local_exp = jnp.where(causal, jnp.exp(local_scores - row_max[..., None]), 0.0)
        total = jnp.sum(prompt_exp, axis=-1) + jnp.sum(local_exp, axis=-1)
        prompt_probs = prompt_exp / total[..., None]
        local_probs = local_exp / total[..., None]
        prompt_dprobs = jnp.einsum("ntkjd,pkd->ntkjp", grads, pvalues)
        local_dprobs = jnp.einsum("ntkjd,nukd->ntkju", grads, own_values)
        delta = jnp.sum(prompt_probs * prompt_dprobs, axis=-1) + jnp.sum(local_probs * local_dprobs, axis=-1)
        prompt_ds = to_half(prompt_probs * (prompt_dprobs - delta[..., None]))
        local_ds = to_half(local_probs * (local_dprobs - delta[..., None]))
        prompt_half = to_half(prompt_probs)
        local_half = to_half(local_probs)
        grad_q = softmax_scale * (jnp.einsum("ntkjp,pkd->ntkjd", prompt_ds, pkeys)
                                  + jnp.einsum("ntkju,nukd->ntkjd", local_ds, own_keys))
        grad_pkeys = softmax_scale * jnp.einsum("ntkjp,ntkjd->pkd", prompt_ds, query)
        grad_pvalues = jnp.einsum("ntkjp,ntkjd->pkd", prompt_half, grads)
        grad_okeys = softmax_scale * jnp.einsum("ntkju,ntkjd->nukd", local_ds, query)
        grad_ovalues = jnp.einsum("ntkju,ntkjd->nukd", local_half, grads)
        return (grad_q.reshape(GROUP, RT, QH * HD).astype(jnp.bfloat16),
                grad_okeys.reshape(GROUP, RT, KVH * HD).astype(jnp.bfloat16),
                grad_ovalues.reshape(GROUP, RT, KVH * HD).astype(jnp.bfloat16),
                grad_pkeys.reshape(PLEN, KVH * HD).astype(jnp.bfloat16),
                grad_pvalues.reshape(PLEN, KVH * HD).astype(jnp.bfloat16))

    results = lax.map(one_prompt, (jnp.arange(N_ROLL, dtype=jnp.int32), members))
    flat_members = members.reshape(-1)
    grad_query = jnp.zeros((TSLOTS, RT, QH * HD), jnp.bfloat16).at[flat_members].set(results[0].reshape(-1, RT, QH * HD))
    grad_roll_keys = jnp.zeros((TSLOTS, RT, KVH * HD), jnp.bfloat16).at[flat_members].set(results[1].reshape(-1, RT, KVH * HD))
    grad_roll_values = jnp.zeros((TSLOTS, RT, KVH * HD), jnp.bfloat16).at[flat_members].set(results[2].reshape(-1, RT, KVH * HD))
    grad_prompt_keys = jnp.zeros((N_ROLL, PLEN, KVH * HD), jnp.bfloat16).at[prompt_owner].set(results[3]).reshape(N_ROLL * PLEN, KVH * HD)
    grad_prompt_values = jnp.zeros((N_ROLL, PLEN, KVH * HD), jnp.bfloat16).at[prompt_owner].set(results[4]).reshape(N_ROLL * PLEN, KVH * HD)
    return grad_query, grad_roll_keys, grad_roll_values, grad_prompt_keys, grad_prompt_values
```

```python
import jax
import jax.numpy as jnp
from jax import lax
from jax.experimental import pallas as pl
from jax.experimental.pallas import tpu as pltpu
from jax.sharding import PartitionSpec as P

HD = 128
GROUP = 16


def slot_tables(slot_prompt, prompt_owner, roll_count, slot_count, bucket_cap, my_index):
    own_prompt = lax.dynamic_slice_in_dim(slot_prompt, my_index * slot_count, slot_count)
    is_live = own_prompt >= 0
    numbers = jnp.arange(roll_count, dtype=jnp.int32)
    target = jnp.sum(
        jnp.where(own_prompt[:, None] == numbers[None, :], prompt_owner[None, :], 0), axis=1
    )
    slot_ids = jnp.arange(slot_count, dtype=jnp.int32)
    earlier = (own_prompt[None, :] == own_prompt[:, None]) & (slot_ids[None, :] < slot_ids[:, None])
    rank_in = jnp.sum(earlier.astype(jnp.int32), axis=1)
    bucket_at = jnp.where(is_live, target * bucket_cap + rank_in, -1)
    buckets = jnp.arange(roll_count * bucket_cap, dtype=jnp.int32)
    matches = bucket_at[None, :] == buckets[:, None]
    source = jnp.sum(jnp.where(matches, slot_ids[None, :], 0), axis=1)
    filled = jnp.any(matches, axis=1)
    return (bucket_at, is_live, source, filled)


def owner_tables(
    slot_prompt,
    prompt_owner,
    roll_len,
    prompt_len,
    roll_count,
    slot_count,
    bucket_cap,
    my_index,
    group_size,
):
    numbers = jnp.arange(roll_count, dtype=jnp.int32)
    my_prompt = jnp.sum(jnp.where(prompt_owner == my_index, numbers, 0))
    plen_live = jnp.sum(jnp.where(numbers == my_prompt, prompt_len, 0))
    all_slots = jnp.arange(slot_prompt.shape[0], dtype=jnp.int32)
    member = slot_prompt == my_prompt
    counted = jnp.cumsum(member.astype(jnp.int32)) - 1
    ordinal = jnp.arange(group_size, dtype=jnp.int32)
    chosen = member[None, :] & (counted[None, :] == ordinal[:, None])
    picked = jnp.sum(jnp.where(chosen, all_slots[None, :], 0), axis=1)
    device = picked // slot_count
    before = (
        member[None, :]
        & (all_slots[None, :] // slot_count == device[:, None])
        & (all_slots[None, :] < picked[:, None])
    )
    arrival = device * bucket_cap + jnp.sum(before.astype(jnp.int32), axis=1)
    lengths = jnp.sum(jnp.where(chosen, roll_len[None, :], 0), axis=1)
    return (arrival, lengths, plen_live)


def pack_rows(values, source, filled):
    fetched = jnp.take(values, source, axis=0)
    return jnp.where(filled[:, None, None], fetched, jnp.zeros((), values.dtype))


def unpack_rows(values, bucket_at, is_live):
    fetched = jnp.take(values, jnp.maximum(bucket_at, 0), axis=0)
    return jnp.where(is_live[:, None, None], fetched, jnp.zeros((), values.dtype))


def owner_work(q_in, g_in, k_in, v_in, keys, values, arrival, lengths, plen_live, group_size):
    softmax_scale = HD ** (-0.5)
    rows = q_in.shape[1]
    kv_local = keys.shape[1] // HD
    heads_per = q_in.shape[2] // (kv_local * HD)
    plen = keys.shape[0]
    per_block = max(1, min(group_size, 512 // (rows * kv_local * heads_per)))
    while group_size % per_block != 0:
        per_block = per_block - 1
    blocks = group_size // per_block
    tok_pos = jnp.arange(rows, dtype=jnp.int32)
    valid = tok_pos[None, :] < lengths[:, None]
    query = jnp.take(q_in, arrival, axis=0).reshape(
        blocks, per_block, rows, kv_local, heads_per, HD
    )
    grad_rows = jnp.take(g_in, arrival, axis=0)
    grads = jnp.where(valid[:, :, None], grad_rows, jnp.zeros((), grad_rows.dtype)).reshape(
        blocks, per_block, rows, kv_local, heads_per, HD
    )
    own_keys = jnp.take(k_in, arrival, axis=0).reshape(blocks, per_block, rows, kv_local, HD)
    own_values = jnp.take(v_in, arrival, axis=0).reshape(blocks, per_block, rows, kv_local, HD)
    pkeys = keys.reshape(plen, kv_local, HD)
    pvalues = values.reshape(plen, kv_local, HD)
    visible = (jnp.arange(plen, dtype=jnp.int32) < plen_live)[None, None, None, None, :]
    causal = (tok_pos[None, :] <= tok_pos[:, None])[None, :, None, None, :]
    f32 = jnp.float32

    def step(carry, inputs):
        acc_keys, acc_values = carry
        query_b, grads_b, okeys_b, ovalues_b = inputs
        prompt_scores = (
            jnp.einsum("ntkjd,pkd->ntkjp", query_b, pkeys, preferred_element_type=f32)
            * softmax_scale
        )
        local_scores = (
            jnp.einsum("ntkjd,nukd->ntkju", query_b, okeys_b, preferred_element_type=f32)
            * softmax_scale
        )
        row_max = jnp.maximum(
            jnp.max(jnp.where(visible, prompt_scores, -jnp.inf), axis=-1),
            jnp.max(jnp.where(causal, local_scores, -jnp.inf), axis=-1),
        )
        prompt_exp = jnp.where(visible, jnp.exp(prompt_scores - row_max[..., None]), 0.0)
        local_exp = jnp.where(causal, jnp.exp(local_scores - row_max[..., None]), 0.0)
        total = jnp.sum(prompt_exp, axis=-1) + jnp.sum(local_exp, axis=-1)
        prompt_probs = prompt_exp / total[..., None]
        local_probs = local_exp / total[..., None]
        prompt_dprobs = jnp.einsum("ntkjd,pkd->ntkjp", grads_b, pvalues, preferred_element_type=f32)
        local_dprobs = jnp.einsum(
            "ntkjd,nukd->ntkju", grads_b, ovalues_b, preferred_element_type=f32
        )
        delta = jnp.sum(prompt_probs * prompt_dprobs, axis=-1) + jnp.sum(
            local_probs * local_dprobs, axis=-1
        )
        prompt_ds = (prompt_probs * (prompt_dprobs - delta[..., None])).astype(jnp.bfloat16)
        local_ds = (local_probs * (local_dprobs - delta[..., None])).astype(jnp.bfloat16)
        prompt_half = prompt_probs.astype(jnp.bfloat16)
        local_half = local_probs.astype(jnp.bfloat16)
        grad_q = softmax_scale * (
            jnp.einsum("ntkjp,pkd->ntkjd", prompt_ds, pkeys, preferred_element_type=f32)
            + jnp.einsum("ntkju,nukd->ntkjd", local_ds, okeys_b, preferred_element_type=f32)
        )
        acc_keys = acc_keys + softmax_scale * jnp.einsum(
            "ntkjp,ntkjd->pkd", prompt_ds, query_b, preferred_element_type=f32
        )
        acc_values = acc_values + jnp.einsum(
            "ntkjp,ntkjd->pkd", prompt_half, grads_b, preferred_element_type=f32
        )
        grad_okeys = softmax_scale * jnp.einsum(
            "ntkju,ntkjd->nukd", local_ds, query_b, preferred_element_type=f32
        )
        grad_ovalues = jnp.einsum(
            "ntkju,ntkjd->nukd", local_half, grads_b, preferred_element_type=f32
        )
        return (
            (acc_keys, acc_values),
            (
                grad_q.astype(jnp.bfloat16),
                grad_okeys.astype(jnp.bfloat16),
                grad_ovalues.astype(jnp.bfloat16),
            ),
        )

    zeros_acc = jnp.zeros((plen, kv_local, HD), jnp.float32)
    (acc_keys, acc_values), (grad_q, grad_okeys, grad_ovalues) = lax.scan(
        step, (zeros_acc, zeros_acc), (query, grads, own_keys, own_values)
    )
    bucket_rows = q_in.shape[0]
    grad_q = grad_q.reshape(group_size, rows, q_in.shape[2])
    grad_okeys = grad_okeys.reshape(group_size, rows, k_in.shape[2])
    grad_ovalues = grad_ovalues.reshape(group_size, rows, k_in.shape[2])
    q_back = jnp.zeros((bucket_rows, rows, q_in.shape[2]), jnp.bfloat16).at[arrival].set(grad_q)
    k_back = jnp.zeros((bucket_rows, rows, k_in.shape[2]), jnp.bfloat16).at[arrival].set(grad_okeys)
    v_back = (
        jnp.zeros((bucket_rows, rows, k_in.shape[2]), jnp.bfloat16).at[arrival].set(grad_ovalues)
    )
    return (
        q_back,
        k_back,
        v_back,
        acc_keys.reshape(plen, -1).astype(jnp.bfloat16),
        acc_values.reshape(plen, -1).astype(jnp.bfloat16),
    )


def general(
    q_tokens,
    grad_tokens,
    roll_keys,
    roll_values,
    prompt_keys,
    prompt_values,
    slot_prompt,
    prompt_owner,
    roll_len,
    prompt_len,
):
    roll_count = lax.axis_size("roll")
    my_index = lax.axis_index("roll")
    slot_count = q_tokens.shape[0]
    bucket_cap = 2 * ((slot_count // 2 + roll_count - 1) // roll_count)
    bucket_at, is_live, source, filled = slot_tables(
        slot_prompt, prompt_owner, roll_count, slot_count, bucket_cap, my_index
    )
    arrival, lengths, plen_live = owner_tables(
        slot_prompt,
        prompt_owner,
        roll_len,
        prompt_len,
        roll_count,
        slot_count,
        bucket_cap,
        my_index,
        GROUP,
    )
    q_head, g_head, k_head, v_head = (
        lax.all_to_all(q_tokens, "kv", split_axis=2, concat_axis=1, tiled=True),
        lax.all_to_all(grad_tokens, "kv", split_axis=2, concat_axis=1, tiled=True),
        lax.all_to_all(roll_keys, "kv", split_axis=2, concat_axis=1, tiled=True),
        lax.all_to_all(roll_values, "kv", split_axis=2, concat_axis=1, tiled=True),
    )
    sent_q = pack_rows(q_head, source, filled)
    sent_g = pack_rows(g_head, source, filled)
    sent_k = pack_rows(k_head, source, filled)
    sent_v = pack_rows(v_head, source, filled)
    q_in, g_in, k_in, v_in = (
        lax.all_to_all(sent_q, "roll", split_axis=0, concat_axis=0, tiled=True),
        lax.all_to_all(sent_g, "roll", split_axis=0, concat_axis=0, tiled=True),
        lax.all_to_all(sent_k, "roll", split_axis=0, concat_axis=0, tiled=True),
        lax.all_to_all(sent_v, "roll", split_axis=0, concat_axis=0, tiled=True),
    )
    q_back, k_back, v_back, grad_pkeys, grad_pvalues = owner_work(
        q_in, g_in, k_in, v_in, prompt_keys, prompt_values, arrival, lengths, plen_live, GROUP
    )
    q_home, k_home, v_home = (
        lax.all_to_all(q_back, "roll", split_axis=0, concat_axis=0, tiled=True),
        lax.all_to_all(k_back, "roll", split_axis=0, concat_axis=0, tiled=True),
        lax.all_to_all(v_back, "roll", split_axis=0, concat_axis=0, tiled=True),
    )
    slot_q = unpack_rows(q_home, bucket_at, is_live)
    slot_k = unpack_rows(k_home, bucket_at, is_live)
    slot_v = unpack_rows(v_home, bucket_at, is_live)
    grad_query, grad_okeys, grad_ovalues = (
        lax.all_to_all(slot_q, "kv", split_axis=1, concat_axis=2, tiled=True),
        lax.all_to_all(slot_k, "kv", split_axis=1, concat_axis=2, tiled=True),
        lax.all_to_all(slot_v, "kv", split_axis=1, concat_axis=2, tiled=True),
    )
    return (grad_query, grad_okeys, grad_ovalues, grad_pkeys, grad_pvalues)


CAP = 8
N_KV = 8
N_ROLL = 32
SLOTS = 32
TSLOTS = 1024
RT = 24
PLEN = 2048
HG = 8
ROWS = GROUP * RT
MESH = pl.DeviceIdType.MESH
BF = jnp.bfloat16
F32 = jnp.float32
CHUNK = 64
LANES = CHUNK * HG
KB = 256
WIN = 2 * CHUNK
LOG2E = 1.4426950408889634
VMEM_BYTES = 56 * 1024 * 1024


def dot(a, b):
    return jnp.dot(a, b, preferred_element_type=F32)


def route_tables(slot_prompt, prompt_owner, roll_len, prompt_len, me):
    n = jnp.arange(TSLOTS, dtype=jnp.int32)
    names = jnp.arange(N_ROLL, dtype=jnp.int32)
    live = slot_prompt >= 0
    dest = jnp.sum(
        jnp.where(slot_prompt[:, None] == names[None, :], prompt_owner[None, :] + 1, 0), axis=1
    ) - 1
    src = n // SLOTS
    xs, ys = src // 8, (src // 2) % 4
    xd, yd, cd = dest // 8, (dest // 2) % 4, dest % 2
    chip = xs * 4 + ys
    keys = jnp.stack(
        [
            (chip * 2 + cd) * 4 + xd,
            (chip * 2 + cd) * 4 + yd,
            ((xd * 4 + ys) * 2 + cd) * 4 + yd,
            ((xs * 4 + yd) * 2 + cd) * 4 + xd,
            dest,
        ]
    )
    keys = jnp.where(live[None, :], keys, -1)
    same = (keys[:, None, :] == keys[:, :, None]) & (n[None, None, :] < n[None, :, None])
    rank = jnp.sum(same.astype(jnp.int32), axis=2)
    fits = jnp.max(jnp.where(live[None, :], rank[:4], 0)) < CAP

    x, y, c = me // 8, (me // 2) % 4, me % 2
    first = jnp.where((live & (cd == c))[None, :], jnp.stack([xd, yd]) * CAP + rank[:2], -1)
    own = lax.dynamic_slice_in_dim(first, me * SLOTS, SLOTS, 1)
    other = lax.dynamic_slice_in_dim(first, (me + 1 - 2 * c) * SLOTS, SLOTS, 1)
    first = jnp.concatenate([own, other], axis=1)

    mine = live & (dest == me)
    in_a = live & (ys == y) & (xd == x) & (cd == c)
    in_b = live & (xs == x) & (yd == y) & (cd == c)
    pos = jnp.stack(
        [
            jnp.where(in_a, xs * CAP + rank[0], -1),
            jnp.where(in_b, ys * CAP + rank[1], -1),
            jnp.where(mine, ys * CAP + rank[2], -1),
            jnp.where(mine, xs * CAP + rank[3], -1),
            jnp.where(mine, rank[4], -1),
        ]
    )
    val = jnp.stack([yd * CAP + rank[2], xd * CAP + rank[3], rank[4], rank[4], roll_len - 1])
    places = jnp.arange(32, dtype=jnp.int32)
    picked = jnp.sum(
        jnp.where(pos[:, None, :] == places[None, :, None], val[:, None, :] + 1, 0), axis=2
    ) - 1
    lens = picked[4, :GROUP] + 1

    def spread(code, h):
        return jnp.where(code >= 0, (code // CAP) * 16 + h * CAP + code % CAP, -1)

    second = picked[:2].reshape(2, 4, CAP)
    second = jnp.stack([spread(second, 0), spread(second, 1)], axis=2).reshape(2, 64)
    third = picked[2:4].reshape(2, 4, CAP)
    third = jnp.stack([third, jnp.where(third >= 0, third + GROUP, -1)], axis=2).reshape(2, 64)
    there = jnp.stack([first, second, third])
    back = jnp.stack([spread(first, 0), spread(first, 1), second, third])
    at = jnp.arange(64, dtype=jnp.int32)
    mats = (there[:, :, None, :] == at[None, None, :, None]).astype(BF)
    mats_back = (back[:, :, :, None] == at[None, None, None, :]).astype(BF)
    my_prompt = prompt_owner == me
    plen = jnp.sum(jnp.where(my_prompt, prompt_len, 0)).reshape(1)
    return fits, mats, mats_back, lens, plen


class Place:
    def __init__(self):
        self.kv = lax.axis_index("kv")
        self.me = lax.axis_index("roll")
        self.x = self.me // 8
        self.y = (self.me // 2) % 4
        self.c = self.me % 2

    def pos(self, axis):
        return self.x if axis == 0 else self.y

    def chip(self, axis, step):
        if axis == 0:
            return (self.kv, ((self.x + step) % 4) * 8 + self.y * 2 + self.c)
        return (self.kv, self.x * 8 + ((self.y + step) % 4) * 2 + self.c)

    def core(self):
        return (self.kv, self.x * 8 + self.y * 2 + 1 - self.c)

    def head(self, step):
        return ((self.kv + step) % N_KV, self.me)

    def greet(self):
        peers = [self.core()]
        peers += [self.chip(axis, i) for axis in (0, 1) for i in (1, 2, 3)]
        peers += [self.head(i) for i in range(1, N_KV)]
        barrier = pltpu.get_barrier_semaphore()
        for peer in peers:
            pl.semaphore_signal(barrier, inc=1, device_id=peer, device_id_type=MESH)
        pl.semaphore_wait(barrier, len(peers))


def remote(src, dst, send, recv, peer):
    return pltpu.make_async_remote_copy(
        src_ref=src, dst_ref=dst, send_sem=send, recv_sem=recv, device_id=peer, device_id_type=MESH
    )


def rows16(p):
    return pl.ds(pl.multiple_of(p * 16, 16), 16)


def axis_send(place, axis, out, land, send, recv):
    p = place.pos(axis)
    copies = []
    for i in (1, 2, 3):
        q = (p + i) % 4
        cp = remote(
            out.at[rows16(q)], land.at[rows16(p)], send.at[i - 1], recv.at[i - 1],
            place.chip(axis, i),
        )
        cp.start()
        copies.append(cp)
    land[rows16(p), :] = out[rows16(p), :]
    return copies


def axis_wait(place, axis, out, land, send, recv):
    p = place.pos(axis)
    for i in (1, 2, 3):
        q = (p - i + 4) % 4
        remote(
            out.at[rows16(q)], land.at[rows16(q)], send.at[i - 1], recv.at[i - 1],
            place.chip(axis, i),
        ).wait_recv()


def there_kernel(
    q, g, k, v, mats, qk_out, gv_out,
    cq, cg, ck, cv, s1, r1, s2, r2, s3,
    core_s, core_r, p1_s, p1_r, p2_s, p2_r, z_s, z_r, loc,
):
    place = Place()
    place.greet()
    kv = place.kv
    sent = []
    pairs = ((q, cq), (k, ck), (g, cg), (v, cv))
    arrived = []
    for t in range(3):
        group = []
        for j, (a, b) in enumerate(pairs):
            cp = remote(a.at[t], b.at[t], core_s.at[t, j], core_r.at[t, j], place.core())
            cp.start()
            group.append(cp)
        arrived.append(group)
        sent += group

    def pack(t, h):
        big, bigo, small, smallo = (q, cq, k, ck) if h == 0 else (g, cg, v, cv)
        m = mats[0, h, :32, :]
        dst = s1.at[h, t]

        def put(a, b, lo, hi, at):
            def one(o):
                rows = jnp.concatenate([a[t, :, pl.ds(o, 512)], b[t, :, pl.ds(o, 512)]], axis=0)
                return dot(m, rows).reshape(4, CAP, 512)

            both = jnp.concatenate([one(lo), one(hi)], axis=1).reshape(64, 512)
            dst[:, pl.ds(at, 512)] = both.astype(BF)

        def body(i, _):
            lo = pl.multiple_of(i * 512, 512)
            put(big, bigo, lo, pl.multiple_of(lo + 4096, 512), lo)
            return 0

        lax.fori_loop(0, 8, body, 0)
        put(small, smallo, 0, 512, 4096)

    def turn(t, h):
        m = mats[1, h]

        def body(i, _):
            lanes = pl.ds(pl.multiple_of(i * 512, 512), 512)
            s2[h, t, :, lanes] = dot(m, r1[h, t, :, lanes]).astype(BF)
            return 0

        lax.fori_loop(0, 9, body, 0)

    def finish(t, h):
        m = mats[2, h, :32, :]

        def body(i, _):
            o = dot(m, r2[h, t, :, pl.ds(pl.multiple_of(i * 1024, 1024), 1024)]).astype(BF)
            s3[h, t, i, :, 0:1024] = o[:16]
            s3[h, t, i + 4, :, 0:1024] = o[16:]
            return 0

        lax.fori_loop(0, 4, body, 0)
        o = dot(m, r2[h, t, :, 4096:4608]).astype(BF)
        for i in range(4):
            s3[h, t, i, :, 1024:1152] = o[:16, i * 128 : (i + 1) * 128]
            s3[h, t, i + 4, :, 1024:1152] = o[16:, i * 128 : (i + 1) * 128]

    def step1(t):
        for j in range(4):
            arrived[t][j].wait_recv()
        for h in (0, 1):
            pack(t, h)
            sent.extend(axis_send(place, h, s1.at[h, t], r1.at[h, t], p1_s.at[h, t], p1_r.at[h, t]))

    def step2(t):
        for h in (0, 1):
            axis_wait(place, h, s1.at[h, t], r1.at[h, t], p1_s.at[h, t], p1_r.at[h, t])
            turn(t, h)
            sent.extend(
                axis_send(place, 1 - h, s2.at[h, t], r2.at[h, t], p2_s.at[h, t], p2_r.at[h, t])
            )

    local = []

    def step3(t):
        for h in (0, 1):
            out = qk_out if h == 0 else gv_out
            axis_wait(place, 1 - h, s2.at[h, t], r2.at[h, t], p2_s.at[h, t], p2_r.at[h, t])
            finish(t, h)
            for i in (4, 3, 5, 2, 6, 1, 7):
                c = (kv + i) % N_KV
                cp = remote(
                    s3.at[h, t, c], out.at[3 * kv + t], z_s.at[h, t, i - 1], z_r.at[h, t, i - 1],
                    place.head(i),
                )
                cp.start()
                sent.append(cp)
            cp = pltpu.make_async_copy(s3.at[h, t, kv], out.at[3 * kv + t], loc.at[h, t])
            cp.start()
            local.append(cp)

    step1(0)
    step1(1)
    step2(0)
    step1(2)
    step2(1)
    step3(0)
    step2(2)
    step3(1)
    step3(2)
    for t in range(3):
        for h in (0, 1):
            out = qk_out if h == 0 else gv_out
            for i in range(1, N_KV):
                c = (kv - i + N_KV) % N_KV
                remote(
                    s3.at[h, t, c], out.at[3 * c + t], z_s.at[h, t, i - 1], z_r.at[h, t, i - 1],
                    place.head(i),
                ).wait_recv()
    for cp in local:
        cp.wait()
    for cp in sent:
        cp.wait_send()


def there(q, g, k, v, mats):
    vm = pl.BlockSpec(memory_space=pltpu.VMEM)
    hbm = pl.BlockSpec(memory_space=pl.ANY)
    sem = pltpu.SemaphoreType.DMA
    half = pltpu.VMEM((2, 3, 64, 4608), BF)
    return pl.pallas_call(
        there_kernel,
        out_shape=[jax.ShapeDtypeStruct((RT, GROUP, 1152), BF)] * 2,
        in_specs=[vm] * 5,
        out_specs=[hbm] * 2,
        scratch_shapes=[
            pltpu.VMEM((3, SLOTS, 8192), BF),
            pltpu.VMEM((3, SLOTS, 8192), BF),
            pltpu.VMEM((3, SLOTS, 1024), BF),
            pltpu.VMEM((3, SLOTS, 1024), BF),
            half, half, half, half,
            pltpu.VMEM((2, 3, N_KV, GROUP, 1152), BF),
            sem((3, 4)), sem((3, 4)),
            sem((2, 3, 3)), sem((2, 3, 3)),
            sem((2, 3, 3)), sem((2, 3, 3)),
            sem((2, 3, 7)), sem((2, 3, 7)),
            sem((2, 3)),
        ],
        compiler_params=pltpu.CompilerParams(
            collective_id=0, has_side_effects=True, vmem_limit_bytes=VMEM_BYTES
        ),
        name="there",
    )(q, g, k, v, mats)


def back_kernel(
    d, mats, gq, gk, gv,
    rz, s1, r1, s2, r2, own, snd, rcv,
    z_s, z_r, p1_s, p1_r, p2_s, p2_r, core_s, core_r,
):
    place = Place()
    place.greet()
    kv = place.kv
    sent = []
    for t in range(3):
        for i in (4, 3, 5, 2, 6, 1, 7):
            c = (kv + i) % N_KV
            cp = remote(
                d.at[3 * c + t], rz.at[kv, t], z_s.at[t, i - 1], z_r.at[t, i - 1], place.head(i)
            )
            cp.start()
            sent.append(cp)
        rz[kv, t] = d[3 * kv + t]

    def open_up(t, h):
        m = mats[3, h, :, :32]
        for lo in (0, 1):
            def body(i, _):
                lanes = pl.ds(pl.multiple_of(i * 640, 128), 640)
                rows = jnp.concatenate(
                    [rz[h * 4 + lo, t, :, lanes], rz[h * 4 + 2 + lo, t, :, lanes]], axis=0
                )
                to = pl.ds(pl.multiple_of(lo * 1280 + i * 640, 128), 640)
                s1[h, t, :, to] = dot(m, rows).astype(BF)
                return 0

            lax.fori_loop(0, 2, body, 0)

    def turn(t, h):
        m = mats[2, h]

        def body(i, _):
            lanes = pl.ds(pl.multiple_of(i * 512, 512), 512)
            s2[h, t, :, lanes] = dot(m, r1[h, t, :, lanes]).astype(BF)
            return 0

        lax.fori_loop(0, 5, body, 0)

    def close(t, h):
        for hh in (0, 1):
            m = mats[hh, h]

            def body(i, _):
                o = dot(m, r2[h, t, :, pl.ds(pl.multiple_of(i * 640, 128), 640)]).astype(BF)
                c = h * 4 + hh * 2 + i // 2
                lanes = pl.ds(pl.multiple_of((i % 2) * 640, 128), 640)
                own[t, c, :, lanes] = o[:32]
                snd[t, c, :, lanes] = o[32:]
                return 0

            lax.fori_loop(0, 4, body, 0)

    def step1(t):
        for i in range(1, N_KV):
            c = (kv - i + N_KV) % N_KV
            remote(
                d.at[3 * c + t], rz.at[c, t], z_s.at[t, i - 1], z_r.at[t, i - 1], place.head(i)
            ).wait_recv()
        for h in (0, 1):
            open_up(t, h)
            sent.extend(
                axis_send(place, 1 - h, s1.at[h, t], r1.at[h, t], p1_s.at[h, t], p1_r.at[h, t])
            )

    def step2(t):
        for h in (0, 1):
            axis_wait(place, 1 - h, s1.at[h, t], r1.at[h, t], p1_s.at[h, t], p1_r.at[h, t])
            turn(t, h)
            sent.extend(axis_send(place, h, s2.at[h, t], r2.at[h, t], p2_s.at[h, t], p2_r.at[h, t]))

    last = []

    def step3(t):
        for h in (0, 1):
            axis_wait(place, h, s2.at[h, t], r2.at[h, t], p2_s.at[h, t], p2_r.at[h, t])
            close(t, h)
            part = pl.ds(4 * h, 4)
            cp = remote(
                snd.at[t, part], rcv.at[t, part], core_s.at[t, h], core_r.at[t, h], place.core()
            )
            cp.start()
            sent.append(cp)
            last.append(cp)

    def step4(t):
        last[2 * t].wait_recv()
        last[2 * t + 1].wait_recv()

        def body(c, _):
            wide = pl.ds(pl.multiple_of(c * 1024, 1024), 1024)
            thin = pl.ds(pl.multiple_of(c * 128, 128), 128)
            gq[t, :, wide] = own[t, c, :, 0:1024] + rcv[t, c, :, 0:1024]
            gk[t, :, thin] = own[t, c, :, 1024:1152] + rcv[t, c, :, 1024:1152]
            gv[t, :, thin] = own[t, c, :, 1152:1280] + rcv[t, c, :, 1152:1280]
            return 0

        lax.fori_loop(0, N_KV, body, 0)

    step1(0)
    step1(1)
    step2(0)
    step2(1)
    step3(0)
    step1(2)
    step2(2)
    step3(1)
    step4(0)
    step4(1)
    step3(2)
    step4(2)
    for cp in sent:
        cp.wait_send()


def back(d, mats):
    vm = pl.BlockSpec(memory_space=pltpu.VMEM)
    sem = pltpu.SemaphoreType.DMA
    half = pltpu.VMEM((2, 3, 64, 2560), BF)
    full = pltpu.VMEM((3, N_KV, SLOTS, 1280), BF)
    return pl.pallas_call(
        back_kernel,
        out_shape=[
            jax.ShapeDtypeStruct((3, SLOTS, 8192), BF),
            jax.ShapeDtypeStruct((3, SLOTS, 1024), BF),
            jax.ShapeDtypeStruct((3, SLOTS, 1024), BF),
        ],
        in_specs=[vm] * 2,
        out_specs=[vm] * 3,
        scratch_shapes=[
            pltpu.VMEM((N_KV, 3, GROUP, 1280), BF),
            half, half, half, half,
            full, full, full,
            sem((3, 7)), sem((3, 7)),
            sem((2, 3, 3)), sem((2, 3, 3)),
            sem((2, 3, 3)), sem((2, 3, 3)),
            sem((3, 2)), sem((3, 2)),
        ],
        compiler_params=pltpu.CompilerParams(
            collective_id=1, has_side_effects=True, vmem_limit_bytes=VMEM_BYTES
        ),
        name="back",
    )(d, mats)


def attend_kernel(
    lens, plen_ref, qk, gv, keys, values, dall, dkeys, dvalues,
    qc, gc, cat, qs, gs, kt, sc, dp, scl, dpl, acck, accv, accok, accov, dqt,
):
    scale = HD ** -0.5
    plen = plen_ref[0]
    ends = []
    total = jnp.int32(0)
    for s in range(GROUP):
        total = total + lens[s]
        ends.append(total)
    starts = [jnp.int32(0)] + ends[:-1]
    chunks = (total + CHUNK - 1) // CHUNK
    blocks = (plen + KB - 1) // KB

    def rank_of(at):
        tok, slot = at // GROUP, at % GROUP
        rank = jnp.full(at.shape, -1, jnp.int32)
        for s in range(GROUP):
            rank = jnp.where((slot == s) & (tok < lens[s]), starts[s] + tok, rank)
        return rank

    def start_of(row):
        first = jnp.zeros(row.shape, jnp.int32)
        for s in range(GROUP):
            first = jnp.where(row >= starts[s], starts[s], first)
        return first

    rank_row = rank_of(lax.broadcasted_iota(jnp.int32, (1, ROWS), 1))
    qc[0:CHUNK, :] = jnp.zeros((CHUNK, 1152), BF)
    gc[0:CHUNK, :] = jnp.zeros((CHUNK, 1152), BF)
    cat[...] = jnp.zeros((ROWS, 1280), BF)
    accok[...] = jnp.zeros_like(accok)
    accov[...] = jnp.zeros_like(accov)
    acck[...] = jnp.zeros_like(acck)
    accv[...] = jnp.zeros_like(accv)

    def compact(i, _):
        at = lax.broadcasted_iota(jnp.int32, (CHUNK, ROWS), 0) + i * CHUNK
        pick = jnp.where(at == rank_row, 1.0, 0.0).astype(BF)
        to = pl.ds(pl.multiple_of(i * CHUNK + CHUNK, CHUNK), CHUNK)
        for lo in range(0, 1152, 384):
            qc[to, lo : lo + 384] = dot(pick, qk[:, lo : lo + 384]).astype(BF)
            gc[to, lo : lo + 384] = dot(pick, gv[:, lo : lo + 384]).astype(BF)
        return 0

    lax.fori_loop(0, chunks, compact, 0)

    def turn_keys(b, _):
        rows = pl.ds(pl.multiple_of(b * KB, KB), KB)
        kt[b] = jnp.transpose(keys[rows, :].astype(F32)).astype(BF)
        return 0

    lax.fori_loop(0, blocks, turn_keys, 0)

    def fold_max(s):
        return jnp.max(s.reshape(s.shape[0] // 8, 8, LANES), axis=0)

    def fold_sum(s):
        return jnp.sum(s.reshape(s.shape[0] // 8, 8, LANES), axis=0)

    def chunk(i, _):
        here = pl.ds(pl.multiple_of(i * CHUNK + CHUNK, CHUNK), CHUNK)
        window = pl.ds(pl.multiple_of(i * CHUNK, CHUNK), WIN)
        for h in range(HG):
            qs[h * CHUNK : (h + 1) * CHUNK, :] = qc[here, h * HD : (h + 1) * HD]
            gs[h * CHUNK : (h + 1) * CHUNK, :] = gc[here, h * HD : (h + 1) * HD]
        q_t = jnp.transpose(qs[...].astype(F32)).astype(BF)
        g_t = jnp.transpose(gs[...].astype(F32)).astype(BF)
        own_k = qc[window, 1024:1152]
        own_v = gc[window, 1024:1152]

        def score(b, m):
            rows = pl.ds(pl.multiple_of(b * KB, KB), KB)
            s = dot(keys[rows, :], q_t)
            seen = lax.broadcasted_iota(jnp.int32, (KB, 1), 0) + b * KB < plen
            s = jnp.where(seen, s, -jnp.inf)
            sc[rows, :] = s
            return jnp.maximum(m, fold_max(s))

        m8 = lax.fori_loop(0, blocks, score, jnp.full((8, LANES), -jnp.inf, F32))
        row = lax.broadcasted_iota(jnp.int32, (1, LANES), 1) % CHUNK + i * CHUNK
        first = start_of(row)
        key = lax.broadcasted_iota(jnp.int32, (WIN, 1), 0) + (i - 1) * CHUNK
        s = jnp.where((key <= row) & (key >= first), dot(own_k, q_t), -jnp.inf)
        scl[...] = s
        m = jnp.max(jnp.maximum(m8, fold_max(s)), axis=0, keepdims=True)
        shift = m * (scale * LOG2E)

        def weigh(s, v):
            e = jnp.exp2(s * (scale * LOG2E) - shift)
            dpv = dot(v, g_t)
            return e, dpv

        def soft(b, carry):
            l, dl = carry
            rows = pl.ds(pl.multiple_of(b * KB, KB), KB)
            e, dpv = weigh(sc[rows, :], values[rows, :])
            sc[rows, :] = e
            dp[rows, :] = dpv
            return l + fold_sum(e), dl + fold_sum(e * dpv)

        zero = jnp.zeros((8, LANES), F32)
        l8, d8 = lax.fori_loop(0, blocks, soft, (zero, zero))
        e, dpv = weigh(scl[...], own_v)
        scl[...] = e
        dpl[...] = dpv
        l = jnp.sum(l8 + fold_sum(e), axis=0, keepdims=True)
        inv = 1.0 / l
        delta = jnp.sum(d8 + fold_sum(e * dpv), axis=0, keepdims=True) * inv
        dqt[...] = jnp.zeros_like(dqt)

        def grads(e, dpv):
            p = e * inv
            ds = p * (dpv - delta)
            return p.astype(BF), ds.astype(BF)

        def grad(b, _):
            rows = pl.ds(pl.multiple_of(b * KB, KB), KB)
            p, ds = grads(sc[rows, :], dp[rows, :])
            accv[rows, :] += dot(p, gs[...])
            acck[rows, :] += dot(ds, qs[...])
            dqt[...] += dot(kt[b], ds)
            return 0

        lax.fori_loop(0, blocks, grad, 0)
        p, ds = grads(scl[...], dpl[...])
        accov[window, :] += dot(p, gs[...])
        accok[window, :] += dot(ds, qs[...])
        k_t = jnp.transpose(own_k.astype(F32)).astype(BF)
        dq = jnp.transpose((dqt[...] + dot(k_t, ds)) * scale).astype(BF)
        out = pl.ds(pl.multiple_of(i * CHUNK, CHUNK), CHUNK)
        for h in range(HG):
            cat[out, h * HD : (h + 1) * HD] = dq[h * CHUNK : (h + 1) * CHUNK, :]
        return 0

    lax.fori_loop(0, chunks, chunk, 0)

    def close(b, _):
        rows = pl.ds(pl.multiple_of(b * KB, KB), KB)
        dkeys[rows, :] = (acck[rows, :] * scale).astype(BF)
        dvalues[rows, :] = accv[rows, :].astype(BF)
        return 0

    lax.fori_loop(0, PLEN // KB, close, 0)
    cat[:, 1024:1152] = (accok[CHUNK:, :] * scale).astype(BF)
    cat[:, 1152:1280] = accov[CHUNK:, :].astype(BF)

    def spread(b, _):
        rows = pl.ds(pl.multiple_of(b * 128, 128), 128)
        rank = rank_of(lax.broadcasted_iota(jnp.int32, (128, 1), 0) + b * 128)
        at = lax.broadcasted_iota(jnp.int32, (128, ROWS), 1)
        pick = jnp.where(at == rank, 1.0, 0.0).astype(BF)
        for lo in range(0, 1280, 256):
            dall[rows, lo : lo + 256] = dot(pick, cat[:, lo : lo + 256]).astype(BF)
        return 0

    lax.fori_loop(0, ROWS // 128, spread, 0)


def attend(lens, plen, qk, gv, keys, values):
    vm = pl.BlockSpec(memory_space=pltpu.VMEM)
    sm = pl.BlockSpec(memory_space=pltpu.SMEM)
    return pl.pallas_call(
        attend_kernel,
        out_shape=[
            jax.ShapeDtypeStruct((ROWS, 1280), BF),
            jax.ShapeDtypeStruct((PLEN, HD), BF),
            jax.ShapeDtypeStruct((PLEN, HD), BF),
        ],
        in_specs=[sm, sm, vm, vm, vm, vm],
        out_specs=[vm] * 3,
        scratch_shapes=[
            pltpu.VMEM((ROWS + CHUNK, 1152), BF),
            pltpu.VMEM((ROWS + CHUNK, 1152), BF),
            pltpu.VMEM((ROWS, 1280), BF),
            pltpu.VMEM((LANES, HD), BF),
            pltpu.VMEM((LANES, HD), BF),
            pltpu.VMEM((PLEN // KB, HD, KB), BF),
            pltpu.VMEM((PLEN, LANES), F32),
            pltpu.VMEM((PLEN, LANES), F32),
            pltpu.VMEM((WIN, LANES), F32),
            pltpu.VMEM((WIN, LANES), F32),
            pltpu.VMEM((PLEN, HD), F32),
            pltpu.VMEM((PLEN, HD), F32),
            pltpu.VMEM((ROWS + CHUNK, HD), F32),
            pltpu.VMEM((ROWS + CHUNK, HD), F32),
            pltpu.VMEM((HD, LANES), F32),
        ],
        compiler_params=pltpu.CompilerParams(vmem_limit_bytes=VMEM_BYTES),
        name="attend",
    )(lens, plen, qk, gv, keys, values)


def fast(q, g, k, v, keys, values, mats, mats_back, lens, plen):
    qk, gv = there(*(jnp.transpose(a, (1, 0, 2)) for a in (q, g, k, v)), mats)
    d, dkeys, dvalues = attend(
        lens, plen, qk.reshape(ROWS, 1152), gv.reshape(ROWS, 1152), keys, values
    )
    gq, gk, gvv = back(d.reshape(RT, GROUP, 1280), mats_back)
    return (*(jnp.transpose(a, (1, 0, 2)) for a in (gq, gk, gvv)), dkeys, dvalues)


def per_device(
    q_tokens, grad_tokens, roll_keys, roll_values, prompt_keys, prompt_values,
    slot_prompt, prompt_owner, roll_len, prompt_len,
):
    me = lax.axis_index("roll")
    fits, mats, mats_back, lens, plen = route_tables(
        slot_prompt, prompt_owner, roll_len, prompt_len, me
    )
    arrays = (q_tokens, grad_tokens, roll_keys, roll_values, prompt_keys, prompt_values)
    return lax.cond(
        fits,
        lambda: fast(*arrays, mats, mats_back, lens, plen),
        lambda: general(*arrays, slot_prompt, prompt_owner, roll_len, prompt_len),
    )


def solution(mesh):
    in_specs = (
        P("roll", "kv", None),
        P("roll", "kv", None),
        P("roll", "kv", None),
        P("roll", "kv", None),
        P("roll", "kv"),
        P("roll", "kv"),
        P(),
        P(),
        P(),
        P(),
    )
    out_specs = (
        P("roll", "kv", None),
        P("roll", "kv", None),
        P("roll", "kv", None),
        P("roll", "kv"),
        P("roll", "kv"),
    )
    return jax.shard_map(
        per_device, mesh=mesh, in_specs=in_specs, out_specs=out_specs, check_vma=False
    )
```

```python
import jax
import jax.numpy as jnp
from jax import lax
from jax.experimental import pallas as pl
from jax.experimental.pallas import tpu as pltpu
from jax.sharding import PartitionSpec as P

HD = 128
GROUP = 16


def slot_tables(slot_prompt, prompt_owner, roll_count, slot_count, bucket_cap, my_index):
    own_prompt = lax.dynamic_slice_in_dim(slot_prompt, my_index * slot_count, slot_count)
    is_live = own_prompt >= 0
    numbers = jnp.arange(roll_count, dtype=jnp.int32)
    target = jnp.sum(
        jnp.where(own_prompt[:, None] == numbers[None, :], prompt_owner[None, :], 0), axis=1
    )
    slot_ids = jnp.arange(slot_count, dtype=jnp.int32)
    earlier = (own_prompt[None, :] == own_prompt[:, None]) & (slot_ids[None, :] < slot_ids[:, None])
    rank_in = jnp.sum(earlier.astype(jnp.int32), axis=1)
    bucket_at = jnp.where(is_live, target * bucket_cap + rank_in, -1)
    buckets = jnp.arange(roll_count * bucket_cap, dtype=jnp.int32)
    matches = bucket_at[None, :] == buckets[:, None]
    source = jnp.sum(jnp.where(matches, slot_ids[None, :], 0), axis=1)
    filled = jnp.any(matches, axis=1)
    return (bucket_at, is_live, source, filled)


def owner_tables(
    slot_prompt,
    prompt_owner,
    roll_len,
    prompt_len,
    roll_count,
    slot_count,
    bucket_cap,
    my_index,
    group_size,
):
    numbers = jnp.arange(roll_count, dtype=jnp.int32)
    my_prompt = jnp.sum(jnp.where(prompt_owner == my_index, numbers, 0))
    plen_live = jnp.sum(jnp.where(numbers == my_prompt, prompt_len, 0))
    all_slots = jnp.arange(slot_prompt.shape[0], dtype=jnp.int32)
    member = slot_prompt == my_prompt
    counted = jnp.cumsum(member.astype(jnp.int32)) - 1
    ordinal = jnp.arange(group_size, dtype=jnp.int32)
    chosen = member[None, :] & (counted[None, :] == ordinal[:, None])
    picked = jnp.sum(jnp.where(chosen, all_slots[None, :], 0), axis=1)
    device = picked // slot_count
    before = (
        member[None, :]
        & (all_slots[None, :] // slot_count == device[:, None])
        & (all_slots[None, :] < picked[:, None])
    )
    arrival = device * bucket_cap + jnp.sum(before.astype(jnp.int32), axis=1)
    lengths = jnp.sum(jnp.where(chosen, roll_len[None, :], 0), axis=1)
    return (arrival, lengths, plen_live)


def pack_rows(values, source, filled):
    fetched = jnp.take(values, source, axis=0)
    return jnp.where(filled[:, None, None], fetched, jnp.zeros((), values.dtype))


def unpack_rows(values, bucket_at, is_live):
    fetched = jnp.take(values, jnp.maximum(bucket_at, 0), axis=0)
    return jnp.where(is_live[:, None, None], fetched, jnp.zeros((), values.dtype))


def owner_work(q_in, g_in, k_in, v_in, keys, values, arrival, lengths, plen_live, group_size):
    softmax_scale = HD ** (-0.5)
    rows = q_in.shape[1]
    kv_local = keys.shape[1] // HD
    heads_per = q_in.shape[2] // (kv_local * HD)
    plen = keys.shape[0]
    per_block = max(1, min(group_size, 512 // (rows * kv_local * heads_per)))
    while group_size % per_block != 0:
        per_block = per_block - 1
    blocks = group_size // per_block
    tok_pos = jnp.arange(rows, dtype=jnp.int32)
    valid = tok_pos[None, :] < lengths[:, None]
    query = jnp.take(q_in, arrival, axis=0).reshape(
        blocks, per_block, rows, kv_local, heads_per, HD
    )
    grad_rows = jnp.take(g_in, arrival, axis=0)
    grads = jnp.where(valid[:, :, None], grad_rows, jnp.zeros((), grad_rows.dtype)).reshape(
        blocks, per_block, rows, kv_local, heads_per, HD
    )
    own_keys = jnp.take(k_in, arrival, axis=0).reshape(blocks, per_block, rows, kv_local, HD)
    own_values = jnp.take(v_in, arrival, axis=0).reshape(blocks, per_block, rows, kv_local, HD)
    pkeys = keys.reshape(plen, kv_local, HD)
    pvalues = values.reshape(plen, kv_local, HD)
    visible = (jnp.arange(plen, dtype=jnp.int32) < plen_live)[None, None, None, None, :]
    causal = (tok_pos[None, :] <= tok_pos[:, None])[None, :, None, None, :]
    f32 = jnp.float32

    def step(carry, inputs):
        acc_keys, acc_values = carry
        query_b, grads_b, okeys_b, ovalues_b = inputs
        prompt_scores = (
            jnp.einsum("ntkjd,pkd->ntkjp", query_b, pkeys, preferred_element_type=f32)
            * softmax_scale
        )
        local_scores = (
            jnp.einsum("ntkjd,nukd->ntkju", query_b, okeys_b, preferred_element_type=f32)
            * softmax_scale
        )
        row_max = jnp.maximum(
            jnp.max(jnp.where(visible, prompt_scores, -jnp.inf), axis=-1),
            jnp.max(jnp.where(causal, local_scores, -jnp.inf), axis=-1),
        )
        prompt_exp = jnp.where(visible, jnp.exp(prompt_scores - row_max[..., None]), 0.0)
        local_exp = jnp.where(causal, jnp.exp(local_scores - row_max[..., None]), 0.0)
        total = jnp.sum(prompt_exp, axis=-1) + jnp.sum(local_exp, axis=-1)
        prompt_probs = prompt_exp / total[..., None]
        local_probs = local_exp / total[..., None]
        prompt_dprobs = jnp.einsum("ntkjd,pkd->ntkjp", grads_b, pvalues, preferred_element_type=f32)
        local_dprobs = jnp.einsum(
            "ntkjd,nukd->ntkju", grads_b, ovalues_b, preferred_element_type=f32
        )
        delta = jnp.sum(prompt_probs * prompt_dprobs, axis=-1) + jnp.sum(
            local_probs * local_dprobs, axis=-1
        )
        prompt_ds = (prompt_probs * (prompt_dprobs - delta[..., None])).astype(jnp.bfloat16)
        local_ds = (local_probs * (local_dprobs - delta[..., None])).astype(jnp.bfloat16)
        prompt_half = prompt_probs.astype(jnp.bfloat16)
        local_half = local_probs.astype(jnp.bfloat16)
        grad_q = softmax_scale * (
            jnp.einsum("ntkjp,pkd->ntkjd", prompt_ds, pkeys, preferred_element_type=f32)
            + jnp.einsum("ntkju,nukd->ntkjd", local_ds, okeys_b, preferred_element_type=f32)
        )
        acc_keys = acc_keys + softmax_scale * jnp.einsum(
            "ntkjp,ntkjd->pkd", prompt_ds, query_b, preferred_element_type=f32
        )
        acc_values = acc_values + jnp.einsum(
            "ntkjp,ntkjd->pkd", prompt_half, grads_b, preferred_element_type=f32
        )
        grad_okeys = softmax_scale * jnp.einsum(
            "ntkju,ntkjd->nukd", local_ds, query_b, preferred_element_type=f32
        )
        grad_ovalues = jnp.einsum(
            "ntkju,ntkjd->nukd", local_half, grads_b, preferred_element_type=f32
        )
        return (
            (acc_keys, acc_values),
            (
                grad_q.astype(jnp.bfloat16),
                grad_okeys.astype(jnp.bfloat16),
                grad_ovalues.astype(jnp.bfloat16),
            ),
        )

    zeros_acc = jnp.zeros((plen, kv_local, HD), jnp.float32)
    (acc_keys, acc_values), (grad_q, grad_okeys, grad_ovalues) = lax.scan(
        step, (zeros_acc, zeros_acc), (query, grads, own_keys, own_values)
    )
    bucket_rows = q_in.shape[0]
    grad_q = grad_q.reshape(group_size, rows, q_in.shape[2])
    grad_okeys = grad_okeys.reshape(group_size, rows, k_in.shape[2])
    grad_ovalues = grad_ovalues.reshape(group_size, rows, k_in.shape[2])
    q_back = jnp.zeros((bucket_rows, rows, q_in.shape[2]), jnp.bfloat16).at[arrival].set(grad_q)
    k_back = jnp.zeros((bucket_rows, rows, k_in.shape[2]), jnp.bfloat16).at[arrival].set(grad_okeys)
    v_back = (
        jnp.zeros((bucket_rows, rows, k_in.shape[2]), jnp.bfloat16).at[arrival].set(grad_ovalues)
    )
    return (
        q_back,
        k_back,
        v_back,
        acc_keys.reshape(plen, -1).astype(jnp.bfloat16),
        acc_values.reshape(plen, -1).astype(jnp.bfloat16),
    )


def general(
    q_tokens,
    grad_tokens,
    roll_keys,
    roll_values,
    prompt_keys,
    prompt_values,
    slot_prompt,
    prompt_owner,
    roll_len,
    prompt_len,
):
    roll_count = lax.axis_size("roll")
    my_index = lax.axis_index("roll")
    slot_count = q_tokens.shape[0]
    bucket_cap = 2 * ((slot_count // 2 + roll_count - 1) // roll_count)
    bucket_at, is_live, source, filled = slot_tables(
        slot_prompt, prompt_owner, roll_count, slot_count, bucket_cap, my_index
    )
    arrival, lengths, plen_live = owner_tables(
        slot_prompt,
        prompt_owner,
        roll_len,
        prompt_len,
        roll_count,
        slot_count,
        bucket_cap,
        my_index,
        GROUP,
    )
    q_head, g_head, k_head, v_head = (
        lax.all_to_all(q_tokens, "kv", split_axis=2, concat_axis=1, tiled=True),
        lax.all_to_all(grad_tokens, "kv", split_axis=2, concat_axis=1, tiled=True),
        lax.all_to_all(roll_keys, "kv", split_axis=2, concat_axis=1, tiled=True),
        lax.all_to_all(roll_values, "kv", split_axis=2, concat_axis=1, tiled=True),
    )
    sent_q = pack_rows(q_head, source, filled)
    sent_g = pack_rows(g_head, source, filled)
    sent_k = pack_rows(k_head, source, filled)
    sent_v = pack_rows(v_head, source, filled)
    q_in, g_in, k_in, v_in = (
        lax.all_to_all(sent_q, "roll", split_axis=0, concat_axis=0, tiled=True),
        lax.all_to_all(sent_g, "roll", split_axis=0, concat_axis=0, tiled=True),
        lax.all_to_all(sent_k, "roll", split_axis=0, concat_axis=0, tiled=True),
        lax.all_to_all(sent_v, "roll", split_axis=0, concat_axis=0, tiled=True),
    )
    q_back, k_back, v_back, grad_pkeys, grad_pvalues = owner_work(
        q_in, g_in, k_in, v_in, prompt_keys, prompt_values, arrival, lengths, plen_live, GROUP
    )
    q_home, k_home, v_home = (
        lax.all_to_all(q_back, "roll", split_axis=0, concat_axis=0, tiled=True),
        lax.all_to_all(k_back, "roll", split_axis=0, concat_axis=0, tiled=True),
        lax.all_to_all(v_back, "roll", split_axis=0, concat_axis=0, tiled=True),
    )
    slot_q = unpack_rows(q_home, bucket_at, is_live)
    slot_k = unpack_rows(k_home, bucket_at, is_live)
    slot_v = unpack_rows(v_home, bucket_at, is_live)
    grad_query, grad_okeys, grad_ovalues = (
        lax.all_to_all(slot_q, "kv", split_axis=1, concat_axis=2, tiled=True),
        lax.all_to_all(slot_k, "kv", split_axis=1, concat_axis=2, tiled=True),
        lax.all_to_all(slot_v, "kv", split_axis=1, concat_axis=2, tiled=True),
    )
    return (grad_query, grad_okeys, grad_ovalues, grad_pkeys, grad_pvalues)


CAP = 8
N_KV = 8
N_ROLL = 32
SLOTS = 32
TSLOTS = 1024
RT = 24
PLEN = 2048
HG = 8
MESH = pl.DeviceIdType.MESH
BF = jnp.bfloat16
F32 = jnp.float32
LANES = 8 * N_KV * HG
KB = 512
OWN = 3 * 8 * N_KV
LOG2E = 1.4426950408889634
VMEM_BYTES = 62 * 1024 * 1024


def dot(a, b):
    return jnp.dot(a, b, preferred_element_type=F32)


def dot_t(a, b):
    return lax.dot_general(a, b, (((1,), (1,)), ((), ())), preferred_element_type=F32)


def tables_kernel(where, owner, prompt_len, slots, lens, mats, mats_back, info):
    me, kv = where[0], where[1]
    x, y, c = me // 8, (me // 2) % 4, me % 2
    row = (1, TSLOTS)
    n = lax.broadcasted_iota(jnp.int32, row, 1)
    prompt = slots[...]
    live = prompt >= 0
    dest = jnp.zeros(row, jnp.int32)
    plen = jnp.int32(0)
    for p in range(N_ROLL):
        dest = jnp.where(prompt == p, owner[p], dest)
        plen = plen + jnp.where(owner[p] == me, prompt_len[p], 0)
    src = n // SLOTS
    xs, ys, cs = src // 8, (src // 2) % 4, src % 2
    xd, yd, cd = dest // 8, (dest // 2) % 4, dest % 2
    chip = xs * 4 + ys
    before = (
        lax.broadcasted_iota(jnp.int32, (128, 128), 0) < lax.broadcasted_iota(jnp.int32, (128, 128), 1)
    )
    both = jnp.concatenate(
        [jnp.where(before, 1.0, 0.0), jnp.ones((128, 128), F32)], axis=1
    ).astype(BF)

    def marks(at, count):
        rows = lax.broadcasted_iota(jnp.int32, (count, TSLOTS), 0)
        return jnp.where(rows == at, 1.0, 0.0)

    def rank_in(key, count):
        mark = marks(jnp.where(live, key, -1), count)
        total = jnp.zeros((count, 128), F32)
        parts = []
        for b in range(TSLOTS // 128):
            m = mark[:, b * 128 : (b + 1) * 128]
            o = dot(m.astype(BF), both)
            parts.append(jnp.sum(m * (o[:, :128] + total), axis=0, keepdims=True))
            total = total + o[:, 128:]
        return jnp.concatenate(parts, axis=1).astype(jnp.int32)

    first = (rank_in((chip * 2 + cd) * 4 + xd, 128), rank_in((chip * 2 + cd) * 4 + yd, 128))
    second = (
        rank_in(((xd * 4 + ys) * 2 + cd) * 4 + yd, 128),
        rank_in(((xs * 4 + yd) * 2 + cd) * 4 + xd, 128),
    )
    last = rank_in(dest, N_ROLL)
    most = jnp.maximum(jnp.maximum(first[0], first[1]), jnp.maximum(second[0], second[1]))
    info[0] = jnp.where(jnp.max(most) < CAP, 1, 0)
    info[1] = plen

    mine = live & (dest == me)
    near = live & (cd == c) & (chip == x * 4 + y)
    seat = n % SLOTS + jnp.where(cs == c, 0, SLOTS)
    seat = marks(jnp.where(near, seat, -1), 64).astype(BF)
    for h in (0, 1):
        s1, s2 = (xs, ys) if h == 0 else (ys, xs)
        d1, d2 = (xd, yd) if h == 0 else (yd, xd)
        mid = live & (cd == c) & ((ys == y) & (xd == x) if h == 0 else (xs == x) & (yd == y))

        def wide(place, rank, ok, part):
            return marks(jnp.where(ok, (place * 2 + part) * CAP + rank, -1), 64).astype(BF)

        mats[h, 0] = dot_t(marks(jnp.where(near, d1 * CAP + first[h], -1), 64).astype(BF), seat).astype(BF)
        turn = jnp.zeros((64, 64), F32)
        turn_back = jnp.zeros((64, 64), F32)
        ends = [jnp.zeros((64, 64), F32)] * 3
        end_back = jnp.zeros((64, 64), F32)
        for part in (0, 1):
            mats_back[h, part] = dot_t(seat, wide(d1, first[h], near, part)).astype(BF)
            a, b = wide(s1, first[h], mid, part), wide(d2, second[h], mid, part)
            turn = turn + dot_t(b, a)
            turn_back = turn_back + dot_t(a, b)
            a = wide(s2, second[h], mine, part)
            b = marks(jnp.where(mine, part * GROUP + last, -1), 64).astype(BF)
            end_back = end_back + dot_t(a, b)
            for t in range(3):
                if h == 0:
                    ends[t] = ends[t] + dot_t(b, a)
                else:
                    valid = mine & (3 * kv + t < lens[...])
                    b = marks(jnp.where(valid, part * GROUP + last, -1), 64).astype(BF)
                    ends[t] = ends[t] + dot_t(b, a)
        mats[h, 1] = turn.astype(BF)
        for t in range(3):
            mats[h, 2 + t] = ends[t].astype(BF)
        mats_back[h, 2] = turn_back.astype(BF)
        mats_back[h, 3] = end_back.astype(BF)


def route_tables(slot_prompt, prompt_owner, roll_len, prompt_len):
    where = jnp.stack([lax.axis_index("roll"), lax.axis_index("kv")]).astype(jnp.int32)
    vm = pl.BlockSpec(memory_space=pltpu.VMEM)
    sm = pl.BlockSpec(memory_space=pltpu.SMEM)
    return pl.pallas_call(
        tables_kernel,
        out_shape=[
            jax.ShapeDtypeStruct((2, 5, 64, 64), BF),
            jax.ShapeDtypeStruct((2, 4, 64, 64), BF),
            jax.ShapeDtypeStruct((2,), jnp.int32),
        ],
        in_specs=[sm, sm, sm, vm, vm],
        out_specs=[vm, vm, sm],
        compiler_params=pltpu.CompilerParams(vmem_limit_bytes=VMEM_BYTES),
        name="tables",
    )(where, prompt_owner, prompt_len, slot_prompt.reshape(1, TSLOTS), roll_len.reshape(1, TSLOTS))


class Place:
    def __init__(self):
        self.kv = lax.axis_index("kv")
        self.me = lax.axis_index("roll")
        self.x = self.me // 8
        self.y = (self.me // 2) % 4
        self.c = self.me % 2

    def pos(self, axis):
        return self.x if axis == 0 else self.y

    def chip(self, axis, step):
        if axis == 0:
            return (self.kv, ((self.x + step) % 4) * 8 + self.y * 2 + self.c)
        return (self.kv, self.x * 8 + ((self.y + step) % 4) * 2 + self.c)

    def core(self):
        return (self.kv, self.x * 8 + self.y * 2 + 1 - self.c)

    def head(self, step):
        return ((self.kv + step) % N_KV, self.me)

    def greet(self):
        peers = [self.core()]
        peers += [self.chip(axis, i) for axis in (0, 1) for i in (1, 2, 3)]
        peers += [self.head(i) for i in range(1, N_KV)]
        barrier = pltpu.get_barrier_semaphore()
        for peer in peers:
            pl.semaphore_signal(barrier, inc=1, device_id=peer, device_id_type=MESH)
        pl.semaphore_wait(barrier, len(peers))


def remote(src, dst, send, recv, peer):
    return pltpu.make_async_remote_copy(
        src_ref=src, dst_ref=dst, send_sem=send, recv_sem=recv, device_id=peer, device_id_type=MESH
    )


def rows16(p):
    return pl.ds(pl.multiple_of(p * 16, 16), 16)


def axis_copies(place, axis, out, land, send, recv):
    p = place.pos(axis)
    return [
        remote(
            out.at[rows16((p + i) % 4)], land.at[rows16(p)], send.at[i - 1], recv.at[i - 1],
            place.chip(axis, i),
        )
        for i in (1, 2, 3)
    ]


def axis_send(place, axis, out, land, send, recv):
    for cp in axis_copies(place, axis, out, land, send, recv):
        cp.start()
    mine = rows16(place.pos(axis))
    land[mine, :] = out[mine, :]


def axis_wait(place, axis, out, land, send, recv):
    p = place.pos(axis)
    for i in (1, 2, 3):
        q = rows16((p - i + 4) % 4)
        remote(
            out.at[q], land.at[q], send.at[i - 1], recv.at[i - 1], place.chip(axis, i)
        ).wait_recv()


def head_copies(place, out, land, send, recv):
    return [
        remote(
            out.at[(place.kv + i) % N_KV], land.at[place.kv], send.at[i - 1], recv.at[i - 1],
            place.head(i),
        )
        for i in (4, 3, 5, 2, 6, 1, 7)
    ]


def head_send(place, out, land, send, recv):
    for cp in head_copies(place, out, land, send, recv):
        cp.start()
    land[place.kv] = out[place.kv]


def head_wait(place, out, land, send, recv):
    for i in range(1, N_KV):
        c = (place.kv - i + N_KV) % N_KV
        remote(
            out.at[c], land.at[c], send.at[i - 1], recv.at[i - 1], place.head(i)
        ).wait_recv()


def mega_kernel(
    info, q, g, k, v, mats, mats_back, keys, values,
    gq, gk, gv, dkeys, dvalues,
    cq, cg, ck, cv,
    s1a, s1b, r1a, r1b, s2a, s2b, r2a, r2b, s3a, s3b, za, zb,
    qs, gs, ko, vo, kt, sc, dp, acck, accv, accok, accov, dqf, da, dl,
    rza, rzl, b1a, b1l, t1a, t1l, b2a, b2l, t2a, t2l, snda, sndl, rcva, rcvl,
    core_s, core_r, p1_s, p1_r, p2_s, p2_r, z_s, z_r,
    y_s, y_r, u1_s, u1_r, u2_s, u2_r, home_s, home_r,
):
    place = Place()
    place.greet()
    scale = HD ** -0.5
    plen = info[1]

    def core_copies(t):
        names = [(q.at[t], cq.at[t], t, 0), (g.at[t], cg.at[t], t, 1)]
        if t == 0:
            names += [(k, ck, 3, 0), (v, cv, 3, 1)]
        return [
            remote(a, b, core_s.at[i, j], core_r.at[i, j], place.core()) for a, b, i, j in names
        ]

    def part(first, rest, t, h):
        return first.at[h] if t == 0 else rest.at[h, t - 1]

    def hop1(t, h):
        return (place, h, part(s1a, s1b, t, h), part(r1a, r1b, t, h), p1_s.at[h, t], p1_r.at[h, t])

    def hop2(t, h):
        return (
            place, 1 - h, part(s2a, s2b, t, h), part(r2a, r2b, t, h), p2_s.at[h, t], p2_r.at[h, t],
        )

    def hop3(t, h):
        return (place, part(s3a, s3b, t, h), part(za, zb, t, h), z_s.at[h, t], z_r.at[h, t])

    def pack(t):
        for cp in core_copies(t):
            cp.wait_recv()
        for h in (0, 1):
            m = mats[h, 0, :32, :]
            dst = part(s1a, s1b, t, h)

            def put(a, b, tt, lo, hi, at):
                def one(o):
                    lanes = pl.ds(o, 512)
                    rows = jnp.concatenate([a[tt, :, lanes], b[tt, :, lanes]], axis=0)
                    return dot(m, rows).reshape(4, CAP, 512)

                both = jnp.concatenate([one(lo), one(hi)], axis=1).reshape(64, 512)
                dst[:, pl.ds(at, 512)] = both.astype(BF)

            big, bigo, small, smallo = (q, cq, k, ck) if h == 0 else (g, cg, v, cv)

            def body(i, _):
                lo = pl.multiple_of(i * 512, 512)
                put(big, bigo, t, lo, pl.multiple_of(lo + 4096, 512), lo)
                return 0

            lax.fori_loop(0, 8, body, 0)
            if t == 0:
                for tt in range(3):
                    put(small, smallo, tt, 0, 512, 4096 + tt * 512)

    def send1(t):
        for h in (0, 1):
            axis_send(*hop1(t, h))

    def apply(m, src, dst):
        def body(i, _):
            lanes = pl.ds(pl.multiple_of(i * 512, 512), 512)
            dst[:, lanes] = dot(m, src[:, lanes]).astype(BF)
            return 0

        lax.fori_loop(0, src.shape[1] // 512, body, 0)

    def turn(t):
        for h in (0, 1):
            axis_wait(*hop1(t, h))
            apply(mats[h, 1], part(r1a, r1b, t, h), part(s2a, s2b, t, h))
            axis_send(*hop2(t, h))

    def finish(t):
        for h in (0, 1):
            axis_wait(*hop2(t, h))
            m = mats[h, 2 + t, :32, :]
            src, dst = part(r2a, r2b, t, h), part(s3a, s3b, t, h)

            def body(i, _):
                o = dot(m, src[:, pl.ds(pl.multiple_of(i * 1024, 1024), 1024)]).astype(BF)
                dst[i, :, 0:1024] = o[:16]
                dst[i + 4, :, 0:1024] = o[16:]
                return 0

            lax.fori_loop(0, 4, body, 0)
            if t == 0:
                for tt in range(3):
                    lo = 4096 + tt * 512
                    at = 1024 + tt * HD
                    o = dot(mats[h, 2 + tt, :32, :], src[:, lo : lo + 512]).astype(BF)
                    for i in range(4):
                        dst[i, :, at : at + HD] = o[:16, i * HD : (i + 1) * HD]
                        dst[i + 4, :, at : at + HD] = o[16:, i * HD : (i + 1) * HD]
            head_send(*hop3(t, h))

    def split(block):
        b = block.astype(F32).reshape(N_KV, 2, 8, HD)
        return b[:, 0].reshape(64, HD).astype(BF), b[:, 1].reshape(64, HD).astype(BF)

    def prepare(t):
        for h in (0, 1):
            head_wait(*hop3(t, h))
            src, dst = part(za, zb, t, h), (qs, gs)[h]
            for j in range(HG):
                a, b = split(src[:, :, j * HD : (j + 1) * HD])
                dst[0, j * 64 : (j + 1) * 64, :] = a
                dst[1, j * 64 : (j + 1) * 64, :] = b
            if t == 0:
                dst = (ko, vo)[h]
                for tt in range(3):
                    at = 1024 + tt * HD
                    a, b = split(src[:, :, at : at + HD])
                    dst[0, tt * 64 : (tt + 1) * 64, :] = a
                    dst[1, tt * 64 : (tt + 1) * 64, :] = b

    def fold_max(s):
        return jnp.max(s.reshape(s.shape[0] // 8, 8, LANES), axis=0)

    def fold_sum(s):
        return jnp.sum(s.reshape(s.shape[0] // 8, 8, LANES), axis=0)

    blocks = [slice(b * KB, (b + 1) * KB) for b in range(PLEN // KB)]
    tail = slice(PLEN, PLEN + OWN)

    def chunk(t, e):
        q_t = jnp.transpose(qs[e].astype(F32)).astype(BF)
        g_t = jnp.transpose(gs[e].astype(F32)).astype(BF)
        m8 = jnp.full((8, LANES), -jnp.inf, F32)
        for b, rows in enumerate(blocks):
            s = dot(keys[rows, :], q_t)
            seen = lax.broadcasted_iota(jnp.int32, (KB, 1), 0) + b * KB < plen
            s = jnp.where(seen, s, -jnp.inf)
            sc[rows, :] = s
            m8 = jnp.maximum(m8, fold_max(s))
        key = lax.broadcasted_iota(jnp.int32, (OWN, 1), 0)
        lane = lax.broadcasted_iota(jnp.int32, (1, LANES), 1)
        key_token = 3 * ((key % 64) // 8) + key // 64
        row_token = 3 * ((lane % 64) // 8) + t
        same = (key % 8 == lane % 8) & (key_token <= row_token)
        s = jnp.where(same, dot(ko[e], q_t), -jnp.inf)
        sc[tail, :] = s
        m8 = jnp.maximum(m8, fold_max(s))
        shift = jnp.max(m8, axis=0, keepdims=True) * (scale * LOG2E)

        l8 = jnp.zeros((8, LANES), F32)
        d8 = jnp.zeros((8, LANES), F32)
        for rows in blocks + [tail]:
            w = jnp.exp2(sc[rows, :] * (scale * LOG2E) - shift)
            d = dot(vo[e] if rows is tail else values[rows, :], g_t)
            sc[rows, :] = w
            dp[rows, :] = d
            l8 = l8 + fold_sum(w)
            d8 = d8 + fold_sum(w * d)
        inv = 1.0 / jnp.sum(l8, axis=0, keepdims=True)
        delta = jnp.sum(d8, axis=0, keepdims=True) * inv

        dq = jnp.zeros((HD, LANES), F32)
        for b, rows in enumerate(blocks + [tail]):
            p = sc[rows, :] * inv
            ds = (p * (dp[rows, :] - delta)).astype(BF)
            p = p.astype(BF)
            if rows is tail:
                accov[e] += dot(p, gs[e])
                accok[e] += dot(ds, qs[e])
                k_t = jnp.transpose(ko[e].astype(F32)).astype(BF)
            else:
                accv[rows, :] += dot(p, gs[e])
                acck[rows, :] += dot(ds, qs[e])
                k_t = kt[b]
            dq = dq + dot(k_t, ds)
        dqf[e] = jnp.transpose(dq * scale)

    def joined(pair):
        a, b = (p.reshape(N_KV, 8, HD) for p in pair)
        return jnp.concatenate([a, b], axis=1).astype(BF)

    def piece(rest, final, t, *at):
        return final.at[at] if t == 2 else rest.at[(t, *at)]

    def back0(t):
        return (
            place, dl if t == 2 else da.at[t], rzl if t == 2 else rza.at[t], y_s.at[t], y_r.at[t],
        )

    def back1(t, h):
        return (
            place, 1 - h, piece(b1a, b1l, t, h), piece(t1a, t1l, t, h), u1_s.at[h, t], u1_r.at[h, t],
        )

    def back2(t, h):
        return (
            place, h, piece(b2a, b2l, t, h), piece(t2a, t2l, t, h), u2_s.at[h, t], u2_r.at[h, t],
        )

    def home(t, h):
        heads = pl.ds(4 * h, 4)
        return remote(
            piece(snda, sndl, t, heads), piece(rcva, rcvl, t, heads),
            home_s.at[t, h], home_r.at[t, h], place.core(),
        )

    def leave(t):
        dst = dl if t == 2 else da.at[t]
        for j in range(HG):
            rows = slice(j * 64, (j + 1) * 64)
            dst[:, :, j * HD : (j + 1) * HD] = joined((dqf[0, rows, :], dqf[1, rows, :]))
        if t == 2:
            for tt in range(3):
                rows = slice(tt * 64, (tt + 1) * 64)
                at = 1024 + tt * HD
                dst[:, :, at : at + HD] = joined((accok[0, rows, :] * scale, accok[1, rows, :] * scale))
                dst[:, :, at + 384 : at + 384 + HD] = joined((accov[0, rows, :], accov[1, rows, :]))
        head_send(*back0(t))

    def open_up(t):
        head_wait(*back0(t))
        src = rzl if t == 2 else rza.at[t]
        wide, step = (1792, 896) if t == 2 else (1024, 512)
        for h in (0, 1):
            m = mats_back[h, 3, :, :32]
            dst = piece(b1a, b1l, t, h)
            for lo in (0, 1):
                for o in range(0, wide, step):
                    rows = jnp.concatenate(
                        [src[h * 4 + lo, :, o : o + step], src[h * 4 + 2 + lo, :, o : o + step]], axis=0
                    )
                    dst[:, lo * wide + o : lo * wide + o + step] = dot(m, rows).astype(BF)
            axis_send(*back1(t, h))

    def turn_back(t):
        for h in (0, 1):
            axis_wait(*back1(t, h))
            apply(mats_back[h, 2], piece(t1a, t1l, t, h), piece(b2a, b2l, t, h))
            axis_send(*back2(t, h))

    def close(t):
        wide = 1792 if t == 2 else 1024
        for h in (0, 1):
            axis_wait(*back2(t, h))
            src = piece(t2a, t2l, t, h)
            for hh in (0, 1):
                m = mats_back[h, hh]
                for lo in (0, 1):
                    c = h * 4 + hh * 2 + lo
                    snd = piece(snda, sndl, t, c)
                    for o in (0, 512):
                        r = dot(m, src[:, lo * wide + o : lo * wide + o + 512]).astype(BF)
                        gq[t, :, c * 1024 + o : c * 1024 + o + 512] = r[:32]
                        snd[:, o : o + 512] = r[32:]
                    if t == 2:
                        r = dot(m, src[:, lo * wide + 1024 : (lo + 1) * wide]).astype(BF)
                        snd[:, 1024:1792] = r[32:]
                        for tt in range(3):
                            lanes = slice(c * HD, (c + 1) * HD)
                            gk[tt, :, lanes] = r[:32, tt * HD : (tt + 1) * HD]
                            gv[tt, :, lanes] = r[:32, 384 + tt * HD : 384 + (tt + 1) * HD]
            home(t, h).start()

    def settle(t):
        for h in (0, 1):
            home(t, h).wait_recv()
        src = rcvl if t == 2 else rcva.at[t]
        for c in range(N_KV):
            lanes = slice(c * 1024, (c + 1) * 1024)
            gq[t, :, lanes] = gq[t, :, lanes] + src[c, :, 0:1024]
            if t == 2:
                lanes = slice(c * HD, (c + 1) * HD)
                for tt in range(3):
                    at = 1024 + tt * HD
                    gk[tt, :, lanes] = gk[tt, :, lanes] + src[c, :, at : at + HD]
                    gv[tt, :, lanes] = gv[tt, :, lanes] + src[c, :, at + 384 : at + 384 + HD]

    for t in range(3):
        for cp in core_copies(t):
            cp.start()
    pack(0)
    send1(0)
    pack(1)
    turn(0)
    send1(1)
    pack(2)
    finish(0)
    turn(1)
    send1(2)
    for b, rows in enumerate(blocks):
        kt[b] = jnp.transpose(keys[rows, :].astype(F32)).astype(BF)
    for ref in (acck, accv, accok, accov):
        ref[...] = jnp.zeros_like(ref)
    finish(1)
    prepare(0)

    def body(i, _):
        chunk(i // 2, i % 2)

        @pl.when(i == 0)
        def _():
            turn(2)

        @pl.when(i == 1)
        def _():
            finish(2)
            leave(0)
            prepare(1)

        @pl.when(i == 3)
        def _():
            leave(1)
            prepare(2)

        @pl.when(i == 4)
        def _():
            open_up(0)

        return 0

    lax.fori_loop(0, 6, body, 0)
    leave(2)
    turn_back(0)
    open_up(1)
    for rows in blocks:
        dkeys[rows, :] = (acck[rows, :] * scale).astype(BF)
        dvalues[rows, :] = accv[rows, :].astype(BF)
    turn_back(1)
    close(0)
    open_up(2)
    close(1)
    settle(0)
    turn_back(2)
    settle(1)
    close(2)
    settle(2)
    for t in range(3):
        for cp in core_copies(t) + head_copies(*back0(t)):
            cp.wait_send()
        for h in (0, 1):
            copies = axis_copies(*hop1(t, h)) + axis_copies(*hop2(t, h)) + head_copies(*hop3(t, h))
            copies += axis_copies(*back1(t, h)) + axis_copies(*back2(t, h)) + [home(t, h)]
            for cp in copies:
                cp.wait_send()


def mega(info, q, g, k, v, mats, mats_back, keys, values):
    vm = pl.BlockSpec(memory_space=pltpu.VMEM)
    sm = pl.BlockSpec(memory_space=pltpu.SMEM)
    sem = pltpu.SemaphoreType.DMA
    bf = lambda *shape: pltpu.VMEM(shape, BF)
    f32 = lambda *shape: pltpu.VMEM(shape, F32)
    there = [bf(2, 64, 5632), bf(2, 2, 64, 4096)]
    back = [bf(2, 2, 64, 2048), bf(2, 64, 3584)]
    home = [bf(2, N_KV, SLOTS, 1024), bf(N_KV, SLOTS, 1792)]
    hop = [sem((2, 3, 3)), sem((2, 3, 3))]
    return pl.pallas_call(
        mega_kernel,
        out_shape=[
            jax.ShapeDtypeStruct((3, SLOTS, 8192), BF),
            jax.ShapeDtypeStruct((3, SLOTS, 1024), BF),
            jax.ShapeDtypeStruct((3, SLOTS, 1024), BF),
            jax.ShapeDtypeStruct((PLEN, HD), BF),
            jax.ShapeDtypeStruct((PLEN, HD), BF),
        ],
        in_specs=[sm] + [vm] * 8,
        out_specs=[vm] * 5,
        scratch_shapes=[
            bf(3, SLOTS, 8192), bf(3, SLOTS, 8192), bf(3, SLOTS, 1024), bf(3, SLOTS, 1024),
            *there, *there, *there, *there,
            bf(2, N_KV, GROUP, 1408), bf(2, 2, N_KV, GROUP, 1024),
            bf(2, N_KV, GROUP, 1408), bf(2, 2, N_KV, GROUP, 1024),
            bf(2, LANES, HD), bf(2, LANES, HD), bf(2, OWN, HD), bf(2, OWN, HD),
            bf(PLEN // KB, HD, KB),
            f32(PLEN + OWN, LANES), f32(PLEN + OWN, LANES),
            f32(PLEN, HD), f32(PLEN, HD), f32(2, OWN, HD), f32(2, OWN, HD),
            f32(2, LANES, HD),
            bf(2, N_KV, GROUP, 1024), bf(N_KV, GROUP, 1792),
            bf(2, N_KV, GROUP, 1024), bf(N_KV, GROUP, 1792),
            *back, *back, *back, *back, *home, *home,
            sem((4, 2)), sem((4, 2)), *hop, *hop, sem((2, 3, 7)), sem((2, 3, 7)),
            sem((3, 7)), sem((3, 7)), *hop, *hop, sem((3, 2)), sem((3, 2)),
        ],
        compiler_params=pltpu.CompilerParams(
            collective_id=0, has_side_effects=True, vmem_limit_bytes=VMEM_BYTES
        ),
        name="mega",
    )(info, q, g, k, v, mats, mats_back, keys, values)


def per_device(
    q_tokens, grad_tokens, roll_keys, roll_values, prompt_keys, prompt_values,
    slot_prompt, prompt_owner, roll_len, prompt_len,
):
    mats, mats_back, info = route_tables(slot_prompt, prompt_owner, roll_len, prompt_len)
    arrays = (q_tokens, grad_tokens, roll_keys, roll_values)

    def direct():
        tokens = (jnp.transpose(a, (1, 0, 2)) for a in arrays)
        gq, gk, gv, dkeys, dvalues = mega(
            info, *tokens, mats, mats_back, prompt_keys, prompt_values
        )
        return (*(jnp.transpose(a, (1, 0, 2)) for a in (gq, gk, gv)), dkeys, dvalues)

    return lax.cond(
        info[0] > 0,
        direct,
        lambda: general(
            *arrays, prompt_keys, prompt_values, slot_prompt, prompt_owner, roll_len, prompt_len
        ),
    )


def solution(mesh):
    in_specs = (
        P("roll", "kv", None),
        P("roll", "kv", None),
        P("roll", "kv", None),
        P("roll", "kv", None),
        P("roll", "kv"),
        P("roll", "kv"),
        P(),
        P(),
        P(),
        P(),
    )
    out_specs = (
        P("roll", "kv", None),
        P("roll", "kv", None),
        P("roll", "kv", None),
        P("roll", "kv"),
        P("roll", "kv"),
    )
    return jax.shard_map(
        per_device, mesh=mesh, in_specs=in_specs, out_specs=out_specs, check_vma=False
    )
```

```python
import jax
import jax.numpy as jnp
from jax import lax
from jax.experimental import pallas as pl
from jax.experimental.pallas import tpu as pltpu
from jax.sharding import PartitionSpec as P

HD = 128
GROUP = 16


def slot_tables(slot_prompt, prompt_owner, roll_count, slot_count, bucket_cap, my_index):
    own_prompt = lax.dynamic_slice_in_dim(slot_prompt, my_index * slot_count, slot_count)
    is_live = own_prompt >= 0
    numbers = jnp.arange(roll_count, dtype=jnp.int32)
    target = jnp.sum(
        jnp.where(own_prompt[:, None] == numbers[None, :], prompt_owner[None, :], 0), axis=1
    )
    slot_ids = jnp.arange(slot_count, dtype=jnp.int32)
    earlier = (own_prompt[None, :] == own_prompt[:, None]) & (slot_ids[None, :] < slot_ids[:, None])
    rank_in = jnp.sum(earlier.astype(jnp.int32), axis=1)
    bucket_at = jnp.where(is_live, target * bucket_cap + rank_in, -1)
    buckets = jnp.arange(roll_count * bucket_cap, dtype=jnp.int32)
    matches = bucket_at[None, :] == buckets[:, None]
    source = jnp.sum(jnp.where(matches, slot_ids[None, :], 0), axis=1)
    filled = jnp.any(matches, axis=1)
    return (bucket_at, is_live, source, filled)


def owner_tables(
    slot_prompt,
    prompt_owner,
    roll_len,
    prompt_len,
    roll_count,
    slot_count,
    bucket_cap,
    my_index,
    group_size,
):
    numbers = jnp.arange(roll_count, dtype=jnp.int32)
    my_prompt = jnp.sum(jnp.where(prompt_owner == my_index, numbers, 0))
    plen_live = jnp.sum(jnp.where(numbers == my_prompt, prompt_len, 0))
    all_slots = jnp.arange(slot_prompt.shape[0], dtype=jnp.int32)
    member = slot_prompt == my_prompt
    counted = jnp.cumsum(member.astype(jnp.int32)) - 1
    ordinal = jnp.arange(group_size, dtype=jnp.int32)
    chosen = member[None, :] & (counted[None, :] == ordinal[:, None])
    picked = jnp.sum(jnp.where(chosen, all_slots[None, :], 0), axis=1)
    device = picked // slot_count
    before = (
        member[None, :]
        & (all_slots[None, :] // slot_count == device[:, None])
        & (all_slots[None, :] < picked[:, None])
    )
    arrival = device * bucket_cap + jnp.sum(before.astype(jnp.int32), axis=1)
    lengths = jnp.sum(jnp.where(chosen, roll_len[None, :], 0), axis=1)
    return (arrival, lengths, plen_live)


def pack_rows(values, source, filled):
    fetched = jnp.take(values, source, axis=0)
    return jnp.where(filled[:, None, None], fetched, jnp.zeros((), values.dtype))


def unpack_rows(values, bucket_at, is_live):
    fetched = jnp.take(values, jnp.maximum(bucket_at, 0), axis=0)
    return jnp.where(is_live[:, None, None], fetched, jnp.zeros((), values.dtype))


def owner_work(q_in, g_in, k_in, v_in, keys, values, arrival, lengths, plen_live, group_size):
    softmax_scale = HD ** (-0.5)
    rows = q_in.shape[1]
    kv_local = keys.shape[1] // HD
    heads_per = q_in.shape[2] // (kv_local * HD)
    plen = keys.shape[0]
    per_block = max(1, min(group_size, 512 // (rows * kv_local * heads_per)))
    while group_size % per_block != 0:
        per_block = per_block - 1
    blocks = group_size // per_block
    tok_pos = jnp.arange(rows, dtype=jnp.int32)
    valid = tok_pos[None, :] < lengths[:, None]
    query = jnp.take(q_in, arrival, axis=0).reshape(
        blocks, per_block, rows, kv_local, heads_per, HD
    )
    grad_rows = jnp.take(g_in, arrival, axis=0)
    grads = jnp.where(valid[:, :, None], grad_rows, jnp.zeros((), grad_rows.dtype)).reshape(
        blocks, per_block, rows, kv_local, heads_per, HD
    )
    own_keys = jnp.take(k_in, arrival, axis=0).reshape(blocks, per_block, rows, kv_local, HD)
    own_values = jnp.take(v_in, arrival, axis=0).reshape(blocks, per_block, rows, kv_local, HD)
    pkeys = keys.reshape(plen, kv_local, HD)
    pvalues = values.reshape(plen, kv_local, HD)
    visible = (jnp.arange(plen, dtype=jnp.int32) < plen_live)[None, None, None, None, :]
    causal = (tok_pos[None, :] <= tok_pos[:, None])[None, :, None, None, :]
    f32 = jnp.float32

    def step(carry, inputs):
        acc_keys, acc_values = carry
        query_b, grads_b, okeys_b, ovalues_b = inputs
        prompt_scores = (
            jnp.einsum("ntkjd,pkd->ntkjp", query_b, pkeys, preferred_element_type=f32)
            * softmax_scale
        )
        local_scores = (
            jnp.einsum("ntkjd,nukd->ntkju", query_b, okeys_b, preferred_element_type=f32)
            * softmax_scale
        )
        row_max = jnp.maximum(
            jnp.max(jnp.where(visible, prompt_scores, -jnp.inf), axis=-1),
            jnp.max(jnp.where(causal, local_scores, -jnp.inf), axis=-1),
        )
        prompt_exp = jnp.where(visible, jnp.exp(prompt_scores - row_max[..., None]), 0.0)
        local_exp = jnp.where(causal, jnp.exp(local_scores - row_max[..., None]), 0.0)
        total = jnp.sum(prompt_exp, axis=-1) + jnp.sum(local_exp, axis=-1)
        prompt_probs = prompt_exp / total[..., None]
        local_probs = local_exp / total[..., None]
        prompt_dprobs = jnp.einsum("ntkjd,pkd->ntkjp", grads_b, pvalues, preferred_element_type=f32)
        local_dprobs = jnp.einsum(
            "ntkjd,nukd->ntkju", grads_b, ovalues_b, preferred_element_type=f32
        )
        delta = jnp.sum(prompt_probs * prompt_dprobs, axis=-1) + jnp.sum(
            local_probs * local_dprobs, axis=-1
        )
        prompt_ds = (prompt_probs * (prompt_dprobs - delta[..., None])).astype(jnp.bfloat16)
        local_ds = (local_probs * (local_dprobs - delta[..., None])).astype(jnp.bfloat16)
        prompt_half = prompt_probs.astype(jnp.bfloat16)
        local_half = local_probs.astype(jnp.bfloat16)
        grad_q = softmax_scale * (
            jnp.einsum("ntkjp,pkd->ntkjd", prompt_ds, pkeys, preferred_element_type=f32)
            + jnp.einsum("ntkju,nukd->ntkjd", local_ds, okeys_b, preferred_element_type=f32)
        )
        acc_keys = acc_keys + softmax_scale * jnp.einsum(
            "ntkjp,ntkjd->pkd", prompt_ds, query_b, preferred_element_type=f32
        )
        acc_values = acc_values + jnp.einsum(
            "ntkjp,ntkjd->pkd", prompt_half, grads_b, preferred_element_type=f32
        )
        grad_okeys = softmax_scale * jnp.einsum(
            "ntkju,ntkjd->nukd", local_ds, query_b, preferred_element_type=f32
        )
        grad_ovalues = jnp.einsum(
            "ntkju,ntkjd->nukd", local_half, grads_b, preferred_element_type=f32
        )
        return (
            (acc_keys, acc_values),
            (
                grad_q.astype(jnp.bfloat16),
                grad_okeys.astype(jnp.bfloat16),
                grad_ovalues.astype(jnp.bfloat16),
            ),
        )

    zeros_acc = jnp.zeros((plen, kv_local, HD), jnp.float32)
    (acc_keys, acc_values), (grad_q, grad_okeys, grad_ovalues) = lax.scan(
        step, (zeros_acc, zeros_acc), (query, grads, own_keys, own_values)
    )
    bucket_rows = q_in.shape[0]
    grad_q = grad_q.reshape(group_size, rows, q_in.shape[2])
    grad_okeys = grad_okeys.reshape(group_size, rows, k_in.shape[2])
    grad_ovalues = grad_ovalues.reshape(group_size, rows, k_in.shape[2])
    q_back = jnp.zeros((bucket_rows, rows, q_in.shape[2]), jnp.bfloat16).at[arrival].set(grad_q)
    k_back = jnp.zeros((bucket_rows, rows, k_in.shape[2]), jnp.bfloat16).at[arrival].set(grad_okeys)
    v_back = (
        jnp.zeros((bucket_rows, rows, k_in.shape[2]), jnp.bfloat16).at[arrival].set(grad_ovalues)
    )
    return (
        q_back,
        k_back,
        v_back,
        acc_keys.reshape(plen, -1).astype(jnp.bfloat16),
        acc_values.reshape(plen, -1).astype(jnp.bfloat16),
    )


def general(
    q_tokens,
    grad_tokens,
    roll_keys,
    roll_values,
    prompt_keys,
    prompt_values,
    slot_prompt,
    prompt_owner,
    roll_len,
    prompt_len,
):
    roll_count = lax.axis_size("roll")
    my_index = lax.axis_index("roll")
    slot_count = q_tokens.shape[0]
    bucket_cap = 2 * ((slot_count // 2 + roll_count - 1) // roll_count)
    bucket_at, is_live, source, filled = slot_tables(
        slot_prompt, prompt_owner, roll_count, slot_count, bucket_cap, my_index
    )
    arrival, lengths, plen_live = owner_tables(
        slot_prompt,
        prompt_owner,
        roll_len,
        prompt_len,
        roll_count,
        slot_count,
        bucket_cap,
        my_index,
        GROUP,
    )
    q_head, g_head, k_head, v_head = (
        lax.all_to_all(q_tokens, "kv", split_axis=2, concat_axis=1, tiled=True),
        lax.all_to_all(grad_tokens, "kv", split_axis=2, concat_axis=1, tiled=True),
        lax.all_to_all(roll_keys, "kv", split_axis=2, concat_axis=1, tiled=True),
        lax.all_to_all(roll_values, "kv", split_axis=2, concat_axis=1, tiled=True),
    )
    sent_q = pack_rows(q_head, source, filled)
    sent_g = pack_rows(g_head, source, filled)
    sent_k = pack_rows(k_head, source, filled)
    sent_v = pack_rows(v_head, source, filled)
    q_in, g_in, k_in, v_in = (
        lax.all_to_all(sent_q, "roll", split_axis=0, concat_axis=0, tiled=True),
        lax.all_to_all(sent_g, "roll", split_axis=0, concat_axis=0, tiled=True),
        lax.all_to_all(sent_k, "roll", split_axis=0, concat_axis=0, tiled=True),
        lax.all_to_all(sent_v, "roll", split_axis=0, concat_axis=0, tiled=True),
    )
    q_back, k_back, v_back, grad_pkeys, grad_pvalues = owner_work(
        q_in, g_in, k_in, v_in, prompt_keys, prompt_values, arrival, lengths, plen_live, GROUP
    )
    q_home, k_home, v_home = (
        lax.all_to_all(q_back, "roll", split_axis=0, concat_axis=0, tiled=True),
        lax.all_to_all(k_back, "roll", split_axis=0, concat_axis=0, tiled=True),
        lax.all_to_all(v_back, "roll", split_axis=0, concat_axis=0, tiled=True),
    )
    slot_q = unpack_rows(q_home, bucket_at, is_live)
    slot_k = unpack_rows(k_home, bucket_at, is_live)
    slot_v = unpack_rows(v_home, bucket_at, is_live)
    grad_query, grad_okeys, grad_ovalues = (
        lax.all_to_all(slot_q, "kv", split_axis=1, concat_axis=2, tiled=True),
        lax.all_to_all(slot_k, "kv", split_axis=1, concat_axis=2, tiled=True),
        lax.all_to_all(slot_v, "kv", split_axis=1, concat_axis=2, tiled=True),
    )
    return (grad_query, grad_okeys, grad_ovalues, grad_pkeys, grad_pvalues)


CAP = 8
N_KV = 8
N_ROLL = 32
SLOTS = 32
TSLOTS = 1024
RT = 24
PLEN = 2048
HG = 8
MESH = pl.DeviceIdType.MESH
BF = jnp.bfloat16
F32 = jnp.float32
LANES = GROUP * N_KV * HG // 2
KB = 512
OWN = RT * GROUP
OWN_UNIT = 6
LOG2E = 1.4426950408889634
VMEM_BYTES = 62 * 1024 * 1024


def dot(a, b):
    return jnp.dot(a, b, preferred_element_type=F32)


def dot_t(a, b):
    return lax.dot_general(a, b, (((1,), (1,)), ((), ())), preferred_element_type=F32)


def tables_kernel(where, owner, prompt_len, slots, lens, mats, mats_back, info):
    me, kv = where[0], where[1]
    x, y, c = me // 8, (me // 2) % 4, me % 2
    row = (1, TSLOTS)
    n = lax.broadcasted_iota(jnp.int32, row, 1)
    prompt = slots[...]
    live = prompt >= 0
    dest = jnp.zeros(row, jnp.int32)
    plen = jnp.int32(0)
    for p in range(N_ROLL):
        dest = jnp.where(prompt == p, owner[p], dest)
        plen = plen + jnp.where(owner[p] == me, prompt_len[p], 0)
    src = n // SLOTS
    xs, ys, cs = src // 8, (src // 2) % 4, src % 2
    xd, yd, cd = dest // 8, (dest // 2) % 4, dest % 2
    chip = xs * 4 + ys
    before = (
        lax.broadcasted_iota(jnp.int32, (128, 128), 0) < lax.broadcasted_iota(jnp.int32, (128, 128), 1)
    )
    both = jnp.concatenate(
        [jnp.where(before, 1.0, 0.0), jnp.ones((128, 128), F32)], axis=1
    ).astype(BF)

    def marks(at, count):
        rows = lax.broadcasted_iota(jnp.int32, (count, TSLOTS), 0)
        return jnp.where(rows == at, 1.0, 0.0)

    def rank_in(key, count):
        mark = marks(jnp.where(live, key, -1), count)
        total = jnp.zeros((count, 128), F32)
        parts = []
        for b in range(TSLOTS // 128):
            m = mark[:, b * 128 : (b + 1) * 128]
            o = dot(m.astype(BF), both)
            parts.append(jnp.sum(m * (o[:, :128] + total), axis=0, keepdims=True))
            total = total + o[:, 128:]
        return jnp.concatenate(parts, axis=1).astype(jnp.int32)

    first = (rank_in((chip * 2 + cd) * 4 + xd, 128), rank_in((chip * 2 + cd) * 4 + yd, 128))
    second = (
        rank_in(((xd * 4 + ys) * 2 + cd) * 4 + yd, 128),
        rank_in(((xs * 4 + yd) * 2 + cd) * 4 + xd, 128),
    )
    last = rank_in(dest, N_ROLL)
    most = jnp.maximum(jnp.maximum(first[0], first[1]), jnp.maximum(second[0], second[1]))
    info[0] = jnp.where(jnp.max(most) < CAP, 1, 0)
    info[1] = plen

    mine = live & (dest == me)
    near = live & (cd == c) & (chip == x * 4 + y)
    seat = n % SLOTS + jnp.where(cs == c, 0, SLOTS)
    seat = marks(jnp.where(near, seat, -1), 64).astype(BF)
    for h in (0, 1):
        s1, s2 = (xs, ys) if h == 0 else (ys, xs)
        d1, d2 = (xd, yd) if h == 0 else (yd, xd)
        mid = live & (cd == c) & ((ys == y) & (xd == x) if h == 0 else (xs == x) & (yd == y))

        def wide(place, rank, ok, part):
            return marks(jnp.where(ok, (place * 2 + part) * CAP + rank, -1), 64).astype(BF)

        mats[h, 0] = dot_t(marks(jnp.where(near, d1 * CAP + first[h], -1), 64).astype(BF), seat).astype(BF)
        turn = jnp.zeros((64, 64), F32)
        turn_back = jnp.zeros((64, 64), F32)
        ends = [jnp.zeros((64, 64), F32)] * 3
        end_back = jnp.zeros((64, 64), F32)
        for part in (0, 1):
            mats_back[h, part] = dot_t(seat, wide(d1, first[h], near, part)).astype(BF)
            a, b = wide(s1, first[h], mid, part), wide(d2, second[h], mid, part)
            turn = turn + dot_t(b, a)
            turn_back = turn_back + dot_t(a, b)
            a = wide(s2, second[h], mine, part)
            b = marks(jnp.where(mine, part * GROUP + last, -1), 64).astype(BF)
            end_back = end_back + dot_t(a, b)
            for t in range(3):
                if h == 0:
                    ends[t] = ends[t] + dot_t(b, a)
                else:
                    valid = mine & (3 * kv + t < lens[...])
                    b = marks(jnp.where(valid, part * GROUP + last, -1), 64).astype(BF)
                    ends[t] = ends[t] + dot_t(b, a)
        mats[h, 1] = turn.astype(BF)
        for t in range(3):
            mats[h, 2 + t] = ends[t].astype(BF)
        mats_back[h, 2] = turn_back.astype(BF)
        mats_back[h, 3] = end_back.astype(BF)


def route_tables(slot_prompt, prompt_owner, roll_len, prompt_len):
    where = jnp.stack([lax.axis_index("roll"), lax.axis_index("kv")]).astype(jnp.int32)
    vm = pl.BlockSpec(memory_space=pltpu.VMEM)
    sm = pl.BlockSpec(memory_space=pltpu.SMEM)
    return pl.pallas_call(
        tables_kernel,
        out_shape=[
            jax.ShapeDtypeStruct((2, 5, 64, 64), BF),
            jax.ShapeDtypeStruct((2, 4, 64, 64), BF),
            jax.ShapeDtypeStruct((2,), jnp.int32),
        ],
        in_specs=[sm, sm, sm, vm, vm],
        out_specs=[vm, vm, sm],
        compiler_params=pltpu.CompilerParams(vmem_limit_bytes=VMEM_BYTES),
        name="tables",
    )(where, prompt_owner, prompt_len, slot_prompt.reshape(1, TSLOTS), roll_len.reshape(1, TSLOTS))


class Place:
    def __init__(self):
        self.kv = lax.axis_index("kv")
        self.me = lax.axis_index("roll")
        self.x = self.me // 8
        self.y = (self.me // 2) % 4
        self.c = self.me % 2

    def pos(self, axis):
        return self.x if axis == 0 else self.y

    def chip(self, axis, step):
        if axis == 0:
            return (self.kv, ((self.x + step) % 4) * 8 + self.y * 2 + self.c)
        return (self.kv, self.x * 8 + ((self.y + step) % 4) * 2 + self.c)

    def core(self):
        return (self.kv, self.x * 8 + self.y * 2 + 1 - self.c)

    def head(self, step):
        return ((self.kv + step) % N_KV, self.me)

    def greet(self):
        peers = [self.core()]
        peers += [self.chip(axis, i) for axis in (0, 1) for i in (1, 2, 3)]
        peers += [self.head(i) for i in range(1, N_KV)]
        barrier = pltpu.get_barrier_semaphore()
        for peer in peers:
            pl.semaphore_signal(barrier, inc=1, device_id=peer, device_id_type=MESH)
        pl.semaphore_wait(barrier, len(peers))


def remote(src, dst, send, recv, peer):
    return pltpu.make_async_remote_copy(
        src_ref=src, dst_ref=dst, send_sem=send, recv_sem=recv, device_id=peer, device_id_type=MESH
    )


def rows16(p):
    return pl.ds(pl.multiple_of(p * 16, 16), 16)


def axis_copies(place, axis, out, land, send, recv):
    p = place.pos(axis)
    return [
        remote(
            out.at[rows16((p + i) % 4)], land.at[rows16(p)], send.at[i - 1], recv.at[i - 1],
            place.chip(axis, i),
        )
        for i in (1, 2, 3)
    ]


def axis_send(place, axis, out, land, send, recv):
    for cp in axis_copies(place, axis, out, land, send, recv):
        cp.start()
    mine = rows16(place.pos(axis))
    land[mine, :] = out[mine, :]


def axis_wait(place, axis, out, land, send, recv):
    p = place.pos(axis)
    for i in (1, 2, 3):
        q = rows16((p - i + 4) % 4)
        remote(
            out.at[q], land.at[q], send.at[i - 1], recv.at[i - 1], place.chip(axis, i)
        ).wait_recv()


def head_copies(place, out, land, send, recv):
    return [
        remote(
            out.at[(place.kv + i) % N_KV], land.at[place.kv], send.at[i - 1], recv.at[i - 1],
            place.head(i),
        )
        for i in (4, 3, 5, 2, 6, 1, 7)
    ]


def head_send(place, out, land, send, recv):
    for cp in head_copies(place, out, land, send, recv):
        cp.start()
    land[place.kv] = out[place.kv]


def head_wait(place, out, land, send, recv):
    for i in range(1, N_KV):
        c = (place.kv - i + N_KV) % N_KV
        remote(
            out.at[c], land.at[c], send.at[i - 1], recv.at[i - 1], place.head(i)
        ).wait_recv()


def mega_kernel(
    info, q, g, k, v, mats, mats_back, keys_in, values_in,
    gq, gk, gv, dkeys, dvalues,
    oq, og, ok, ov, cq, cg, ck, cv, keys, values,
    s1a, s1b, r1a, r1b, s2a, s2b, r2a, r2b, s3, s3s, zu, zs,
    qs, gs, ko, vo, kt, sc, dp, acck, accv, accok, accov, du, dsm, rzu, rzs,
    b1a, b1l, t1a, t1l, b2a, b2l, t2a, t2l, snda, sndl, rcva, rcvl,
    own_s, core_s, core_r, p1_s, p1_r, p2_s, p2_r, z_s, z_r, zs_s, zs_r,
    y_s, y_r, ys_s, ys_r, u1_s, u1_r, u2_s, u2_r, home_s, home_r,
):
    place = Place()
    scale = HD ** -0.5
    plen = info[1]

    def own_copies(t):
        names = [(q.at[t], oq.at[t], t, 0), (g.at[t], og.at[t], t, 1)]
        if t == 0:
            names += [(k, ok, 3, 0), (v, ov, 3, 1)]
        if t == 2:
            names += [(keys_in, keys, 4, 0), (values_in, values, 4, 1)]
        return [pltpu.make_async_copy(a, b, own_s.at[i, j]) for a, b, i, j in names]

    def core_copies(t):
        names = [(q.at[t], cq.at[t], t, 0), (g.at[t], cg.at[t], t, 1)]
        if t == 0:
            names += [(k, ck, 3, 0), (v, cv, 3, 1)]
        return [
            remote(a, b, core_s.at[i, j], core_r.at[i, j], place.core()) for a, b, i, j in names
        ]

    def part(first, rest, u, h):
        return first.at[h] if u == 1 else rest.at[u - (u > 1), h]

    def hop1(u, h):
        return (place, h, part(s1a, s1b, u, h), part(r1a, r1b, u, h), p1_s.at[u, h], p1_r.at[u, h])

    def hop2(u, h):
        return (
            place, 1 - h, part(s2a, s2b, u, h), part(r2a, r2b, u, h), p2_s.at[u, h], p2_r.at[u, h],
        )

    def hop3(u):
        return (place, s3.at[u], zu.at[u], z_s.at[u], z_r.at[u])

    small3 = (place, s3s, zs, zs_s, zs_r)

    def pack(u):
        t, f = u // 2, u % 2
        if f == 0:
            for cp in own_copies(t):
                cp.wait()
            for cp in core_copies(t):
                cp.wait_recv()
        for h in (0, 1):
            m = mats[h, 0, :32, :]
            dst = part(s1a, s1b, u, h)

            def put(a, b, tt, lo, hi, at):
                def one(o):
                    lanes = pl.ds(o, 512)
                    rows = jnp.concatenate([a[tt, :, lanes], b[tt, :, lanes]], axis=0)
                    return dot(m, rows).reshape(4, CAP, 512)

                both = jnp.concatenate([one(lo), one(hi)], axis=1).reshape(64, 512)
                dst[:, pl.ds(at, 512)] = both.astype(BF)

            big, bigo, small, smallo = (oq, cq, ok, ck) if h == 0 else (og, cg, ov, cv)
            for i in range(4):
                lo = i * 1024 + f * 512
                put(big, bigo, t, lo, lo + 4096, i * 512)
            if u == 1:
                for tt in range(3):
                    put(small, smallo, tt, 0, 512, 2048 + tt * 512)

    def send1(u):
        for h in (0, 1):
            axis_send(*hop1(u, h))

    def apply(m, src, dst):
        for o in range(0, src.shape[1], 512):
            dst[:, o : o + 512] = dot(m, src[:, o : o + 512]).astype(BF)

    def turn(u):
        for h in (0, 1):
            axis_wait(*hop1(u, h))
            apply(mats[h, 1], part(r1a, r1b, u, h), part(s2a, s2b, u, h))
            axis_send(*hop2(u, h))

    def finish(u):
        for h in (0, 1):
            axis_wait(*hop2(u, h))
            m = mats[h, 2 + u // 2, :32, :]
            src = part(r2a, r2b, u, h)
            for i in range(4):
                o = dot(m, src[:, i * 512 : (i + 1) * 512]).astype(BF)
                s3[u, i, h] = o[:16]
                s3[u, i + 4, h] = o[16:]
            if u == 1:
                for tt in range(3):
                    lo = 2048 + tt * 512
                    at = slice(tt * HD, (tt + 1) * HD)
                    o = dot(mats[h, 2 + tt, :32, :], src[:, lo : lo + 512]).astype(BF)
                    for i in range(4):
                        s3s[i, h, :, at] = o[:16, i * HD : (i + 1) * HD]
                        s3s[i + 4, h, :, at] = o[16:, i * HD : (i + 1) * HD]
        head_send(*hop3(u))
        if u == 1:
            head_send(*small3)

    def prepare(u):
        head_wait(*hop3(u))
        for h, dst in ((0, qs), (1, gs)):
            for j in range(HG // 2):
                dst[j * 128 : (j + 1) * 128, :] = zu[u, :, h, :, j * HD : (j + 1) * HD].reshape(128, HD)

    def prepare_own():
        head_wait(*small3)
        for h, dst in ((0, ko), (1, vo)):
            for tt in range(3):
                at = slice(tt * 128, (tt + 1) * 128)
                dst[at, :] = zs[:, h, :, at].reshape(128, HD)

    def fold_max(s):
        return jnp.max(s.reshape(s.shape[0] // 8, 8, LANES), axis=0)

    def fold_sum(s):
        return jnp.sum(s.reshape(s.shape[0] // 8, 8, LANES), axis=0)

    blocks = [slice(b * KB, (b + 1) * KB) for b in range(PLEN // KB)]
    tail = slice(PLEN, PLEN + OWN)

    def chunk(u):
        q_t = jnp.transpose(qs[...].astype(F32)).astype(BF)
        g_t = jnp.transpose(gs[...].astype(F32)).astype(BF)
        m8 = jnp.full((8, LANES), -jnp.inf, F32)
        for b, rows in enumerate(blocks):
            s = dot(keys[rows, :], q_t)
            seen = lax.broadcasted_iota(jnp.int32, (KB, 1), 0) + b * KB < plen
            s = jnp.where(seen, s, -jnp.inf)
            sc[rows, :] = s
            m8 = jnp.maximum(m8, fold_max(s))
        key = lax.broadcasted_iota(jnp.int32, (OWN, 1), 0)
        lane = lax.broadcasted_iota(jnp.int32, (1, LANES), 1)
        key_token = 3 * ((key % 128) // GROUP) + key // 128
        row_token = 3 * ((lane % 128) // GROUP) + u // 2
        same = (key % GROUP == lane % GROUP) & (key_token <= row_token)
        s = jnp.where(same, dot(ko[...], q_t), -jnp.inf)
        sc[tail, :] = s
        m8 = jnp.maximum(m8, fold_max(s))
        shift = jnp.max(m8, axis=0, keepdims=True) * (scale * LOG2E)

        l8 = jnp.zeros((8, LANES), F32)
        d8 = jnp.zeros((8, LANES), F32)
        for rows in blocks + [tail]:
            w = jnp.exp2(sc[rows, :] * (scale * LOG2E) - shift)
            d = dot(vo[...] if rows is tail else values[rows, :], g_t)
            sc[rows, :] = w
            dp[rows, :] = d
            l8 = l8 + fold_sum(w)
            d8 = d8 + fold_sum(w * d)
        inv = 1.0 / jnp.sum(l8, axis=0, keepdims=True)
        delta = jnp.sum(d8, axis=0, keepdims=True) * inv

        dq = jnp.zeros((HD, LANES), F32)
        for b, rows in enumerate([tail] + blocks):
            p = sc[rows, :] * inv
            ds = (p * (dp[rows, :] - delta)).astype(BF)
            p = p.astype(BF)
            if rows is tail:
                accov[...] += dot(p, gs[...])
                accok[...] += dot(ds, qs[...])
                k_t = jnp.transpose(ko[...].astype(F32)).astype(BF)
            else:
                accv[rows, :] += dot(p, gs[...])
                acck[rows, :] += dot(ds, qs[...])
                k_t = kt[b - 1]
            dq = dq + dot(k_t, ds)
            if rows is tail:
                pl.when(u == 5)(leave_own)
        dq = jnp.transpose(dq * scale).astype(BF)
        for j in range(HG // 2):
            du[u, :, :, j * HD : (j + 1) * HD] = dq[j * 128 : (j + 1) * 128, :].reshape(N_KV, GROUP, HD)

    def piece(rest, final, u, *at):
        return final.at[at] if u == OWN_UNIT else rest.at[(u, *at)]

    def back0(u):
        return (place, du.at[u], rzu.at[u], y_s.at[u], y_r.at[u])

    small0 = (place, dsm, rzs, ys_s, ys_r)

    def back1(u, h):
        return (
            place, 1 - h, piece(b1a, b1l, u, h), piece(t1a, t1l, u, h), u1_s.at[u, h], u1_r.at[u, h],
        )

    def back2(u, h):
        return (
            place, h, piece(b2a, b2l, u, h), piece(t2a, t2l, u, h), u2_s.at[u, h], u2_r.at[u, h],
        )

    def home(u, h):
        heads = pl.ds(4 * h, 4)
        return remote(
            piece(snda, sndl, u, heads), piece(rcva, rcvl, u, heads),
            home_s.at[u, h], home_r.at[u, h], place.core(),
        )

    def leave_own():
        for tt in range(3):
            at = slice(tt * 128, (tt + 1) * 128)
            dsm[:, :, at] = (accok[at, :] * scale).astype(BF).reshape(N_KV, GROUP, HD)
            dsm[:, :, 384 + tt * 128 : 512 + tt * 128] = accov[at, :].astype(BF).reshape(N_KV, GROUP, HD)
        head_send(*small0)

    def open_up(u):
        head_wait(*(small0 if u == OWN_UNIT else back0(u)))
        src = rzs if u == OWN_UNIT else rzu.at[u]
        wide = src.shape[-1]
        for h in (0, 1):
            m = mats_back[h, 3, :, :32]
            dst = piece(b1a, b1l, u, h)
            for lo in (0, 1):
                rows = jnp.concatenate([src[h * 4 + lo], src[h * 4 + 2 + lo]], axis=0)
                dst[:, lo * wide : (lo + 1) * wide] = dot(m, rows).astype(BF)
            axis_send(*back1(u, h))

    def turn_back(u):
        for h in (0, 1):
            axis_wait(*back1(u, h))
            apply(mats_back[h, 2], piece(t1a, t1l, u, h), piece(b2a, b2l, u, h))
            axis_send(*back2(u, h))

    def close(u):
        t, f = u // 2, u % 2
        for h in (0, 1):
            axis_wait(*back2(u, h))
            src = piece(t2a, t2l, u, h)
            wide = src.shape[-1] // 2
            for hh in (0, 1):
                m = mats_back[h, hh]
                for lo in (0, 1):
                    c = h * 4 + hh * 2 + lo
                    r = dot(m, src[:, lo * wide : (lo + 1) * wide]).astype(BF)
                    piece(snda, sndl, u, c)[...] = r[32:]
                    if u == OWN_UNIT:
                        lanes = slice(c * HD, (c + 1) * HD)
                        for tt in range(3):
                            gk[tt, :, lanes] = r[:32, tt * HD : (tt + 1) * HD]
                            gv[tt, :, lanes] = r[:32, 384 + tt * HD : 384 + (tt + 1) * HD]
                    else:
                        at = c * 1024 + f * 512
                        gq[t, :, at : at + 512] = r[:32]
            home(u, h).start()

    def settle(u):
        t, f = u // 2, u % 2
        for h in (0, 1):
            home(u, h).wait_recv()
        src = rcvl if u == OWN_UNIT else rcva.at[u]
        for c in range(N_KV):
            if u == OWN_UNIT:
                lanes = slice(c * HD, (c + 1) * HD)
                for tt in range(3):
                    at = tt * HD
                    gk[tt, :, lanes] = gk[tt, :, lanes] + src[c, :, at : at + HD]
                    gv[tt, :, lanes] = gv[tt, :, lanes] + src[c, :, at + 384 : at + 384 + HD]
            else:
                lanes = slice(c * 1024 + f * 512, c * 1024 + f * 512 + 512)
                gq[t, :, lanes] = gq[t, :, lanes] + src[c]

    def start(copies):
        for cp in copies:
            cp.start()

    for t in range(3):
        start(own_copies(t))
    place.greet()
    start(core_copies(0))
    pack(0)
    send1(0)
    start(core_copies(1))
    pack(1)
    turn(0)
    send1(1)
    pack(2)
    send1(2)
    start(core_copies(2))
    finish(0)
    turn(1)
    pack(3)
    send1(3)
    finish(1)
    turn(2)
    pack(4)
    send1(4)
    for b, rows in enumerate(blocks):
        kt[b] = jnp.transpose(keys[rows, :].astype(F32)).astype(BF)
    for ref in (acck, accv, accok, accov):
        ref[...] = jnp.zeros_like(ref)
    finish(2)
    turn(3)
    pack(5)
    send1(5)
    prepare_own()

    def body(i, _):
        prepare(i)
        chunk(i)
        head_send(*back0(i))

        @pl.when(i == 0)
        def _():
            finish(3)
            turn(4)

        @pl.when(i == 1)
        def _():
            finish(4)
            turn(5)

        @pl.when(i == 2)
        def _():
            finish(5)
            open_up(0)

        @pl.when(i == 3)
        def _():
            open_up(1)
            turn_back(0)

        @pl.when(i == 4)
        def _():
            open_up(2)
            turn_back(1)
            close(0)

        return 0

    lax.fori_loop(0, 6, body, 0)
    open_up(3)
    turn_back(2)
    close(1)
    open_up(4)
    settle(0)
    turn_back(3)
    close(2)
    settle(1)
    for rows in blocks:
        dkeys[rows, :] = (acck[rows, :] * scale).astype(BF)
        dvalues[rows, :] = accv[rows, :].astype(BF)
    open_up(OWN_UNIT)
    turn_back(4)
    open_up(5)
    turn_back(OWN_UNIT)
    close(3)
    settle(2)
    turn_back(5)
    close(4)
    settle(3)
    close(OWN_UNIT)
    settle(4)
    close(5)
    settle(OWN_UNIT)
    settle(5)
    for t in range(3):
        for cp in core_copies(t):
            cp.wait_send()
    for cp in head_copies(*small3) + head_copies(*small0):
        cp.wait_send()
    for u in range(7):
        copies = []
        if u < 6:
            copies += head_copies(*hop3(u)) + head_copies(*back0(u))
        for h in (0, 1):
            if u < 6:
                copies += axis_copies(*hop1(u, h)) + axis_copies(*hop2(u, h))
            copies += axis_copies(*back1(u, h)) + axis_copies(*back2(u, h)) + [home(u, h)]
        for cp in copies:
            cp.wait_send()


def mega(info, q, g, k, v, mats, mats_back, keys, values):
    vm = pl.BlockSpec(memory_space=pltpu.VMEM)
    sm = pl.BlockSpec(memory_space=pltpu.SMEM)
    hbm = pl.BlockSpec(memory_space=pl.ANY)
    sem = pltpu.SemaphoreType.DMA
    bf = lambda *shape: pltpu.VMEM(shape, BF)
    f32 = lambda *shape: pltpu.VMEM(shape, F32)
    rows = [
        bf(3, SLOTS, 8192), bf(3, SLOTS, 8192), bf(3, SLOTS, 1024), bf(3, SLOTS, 1024),
    ]
    there = [bf(2, 64, 3584), bf(5, 2, 64, 2048)]
    back = [bf(6, 2, 64, 1024), bf(2, 64, 1536)]
    home = [bf(6, N_KV, SLOTS, 512), bf(N_KV, SLOTS, 768)]
    hop_back = [sem((7, 2, 3)), sem((7, 2, 3))]
    hop = [sem((6, 2, 3)), sem((6, 2, 3))]
    head = [sem((6, 7)), sem((6, 7)), sem((7,)), sem((7,))]
    return pl.pallas_call(
        mega_kernel,
        out_shape=[
            jax.ShapeDtypeStruct((3, SLOTS, 8192), BF),
            jax.ShapeDtypeStruct((3, SLOTS, 1024), BF),
            jax.ShapeDtypeStruct((3, SLOTS, 1024), BF),
            jax.ShapeDtypeStruct((PLEN, HD), BF),
            jax.ShapeDtypeStruct((PLEN, HD), BF),
        ],
        in_specs=[sm] + [hbm] * 4 + [vm] * 2 + [hbm] * 2,
        out_specs=[vm] * 5,
        scratch_shapes=[
            *rows, *rows, bf(PLEN, HD), bf(PLEN, HD),
            *there, *there, *there, *there,
            bf(6, N_KV, 2, GROUP, 512), bf(N_KV, 2, GROUP, 384),
            bf(6, N_KV, 2, GROUP, 512), bf(N_KV, 2, GROUP, 384),
            bf(LANES, HD), bf(LANES, HD), bf(OWN, HD), bf(OWN, HD),
            bf(PLEN // KB, HD, KB),
            f32(PLEN + OWN, LANES), f32(PLEN + OWN, LANES),
            f32(PLEN, HD), f32(PLEN, HD), f32(OWN, HD), f32(OWN, HD),
            bf(6, N_KV, GROUP, 512), bf(N_KV, GROUP, 768),
            bf(6, N_KV, GROUP, 512), bf(N_KV, GROUP, 768),
            *back, *back, *back, *back, *home, *home,
            sem((5, 2)), sem((4, 2)), sem((4, 2)), *hop, *hop, *head,
            *head, *hop_back, *hop_back, sem((7, 2)), sem((7, 2)),
        ],
        compiler_params=pltpu.CompilerParams(
            collective_id=0, has_side_effects=True, vmem_limit_bytes=VMEM_BYTES
        ),
        name="mega",
    )(info, q, g, k, v, mats, mats_back, keys, values)


def per_device(
    q_tokens, grad_tokens, roll_keys, roll_values, prompt_keys, prompt_values,
    slot_prompt, prompt_owner, roll_len, prompt_len,
):
    mats, mats_back, info = route_tables(slot_prompt, prompt_owner, roll_len, prompt_len)
    arrays = (q_tokens, grad_tokens, roll_keys, roll_values)

    def direct():
        tokens = (jnp.transpose(a, (1, 0, 2)) for a in arrays)
        gq, gk, gv, dkeys, dvalues = mega(
            info, *tokens, mats, mats_back, prompt_keys, prompt_values
        )
        return (*(jnp.transpose(a, (1, 0, 2)) for a in (gq, gk, gv)), dkeys, dvalues)

    return lax.cond(
        info[0] > 0,
        direct,
        lambda: general(
            *arrays, prompt_keys, prompt_values, slot_prompt, prompt_owner, roll_len, prompt_len
        ),
    )


def solution(mesh):
    in_specs = (
        P("roll", "kv", None),
        P("roll", "kv", None),
        P("roll", "kv", None),
        P("roll", "kv", None),
        P("roll", "kv"),
        P("roll", "kv"),
        P(),
        P(),
        P(),
        P(),
    )
    out_specs = (
        P("roll", "kv", None),
        P("roll", "kv", None),
        P("roll", "kv", None),
        P("roll", "kv"),
        P("roll", "kv"),
    )
    return jax.shard_map(
        per_device, mesh=mesh, in_specs=in_specs, out_specs=out_specs, check_vma=False
    )
```

```python
import jax
import jax.numpy as jnp
from jax import lax
from jax.experimental import pallas as pl
from jax.experimental.pallas import tpu as pltpu
from jax.sharding import PartitionSpec as P

HD = 128
GROUP = 16


def slot_tables(slot_prompt, prompt_owner, roll_count, slot_count, bucket_cap, my_index):
    own_prompt = lax.dynamic_slice_in_dim(slot_prompt, my_index * slot_count, slot_count)
    is_live = own_prompt >= 0
    numbers = jnp.arange(roll_count, dtype=jnp.int32)
    target = jnp.sum(
        jnp.where(own_prompt[:, None] == numbers[None, :], prompt_owner[None, :], 0), axis=1
    )
    slot_ids = jnp.arange(slot_count, dtype=jnp.int32)
    earlier = (own_prompt[None, :] == own_prompt[:, None]) & (slot_ids[None, :] < slot_ids[:, None])
    rank_in = jnp.sum(earlier.astype(jnp.int32), axis=1)
    bucket_at = jnp.where(is_live, target * bucket_cap + rank_in, -1)
    buckets = jnp.arange(roll_count * bucket_cap, dtype=jnp.int32)
    matches = bucket_at[None, :] == buckets[:, None]
    source = jnp.sum(jnp.where(matches, slot_ids[None, :], 0), axis=1)
    filled = jnp.any(matches, axis=1)
    return (bucket_at, is_live, source, filled)


def owner_tables(
    slot_prompt,
    prompt_owner,
    roll_len,
    prompt_len,
    roll_count,
    slot_count,
    bucket_cap,
    my_index,
    group_size,
):
    numbers = jnp.arange(roll_count, dtype=jnp.int32)
    my_prompt = jnp.sum(jnp.where(prompt_owner == my_index, numbers, 0))
    plen_live = jnp.sum(jnp.where(numbers == my_prompt, prompt_len, 0))
    all_slots = jnp.arange(slot_prompt.shape[0], dtype=jnp.int32)
    member = slot_prompt == my_prompt
    counted = jnp.cumsum(member.astype(jnp.int32)) - 1
    ordinal = jnp.arange(group_size, dtype=jnp.int32)
    chosen = member[None, :] & (counted[None, :] == ordinal[:, None])
    picked = jnp.sum(jnp.where(chosen, all_slots[None, :], 0), axis=1)
    device = picked // slot_count
    before = (
        member[None, :]
        & (all_slots[None, :] // slot_count == device[:, None])
        & (all_slots[None, :] < picked[:, None])
    )
    arrival = device * bucket_cap + jnp.sum(before.astype(jnp.int32), axis=1)
    lengths = jnp.sum(jnp.where(chosen, roll_len[None, :], 0), axis=1)
    return (arrival, lengths, plen_live)


def pack_rows(values, source, filled):
    fetched = jnp.take(values, source, axis=0)
    return jnp.where(filled[:, None, None], fetched, jnp.zeros((), values.dtype))


def unpack_rows(values, bucket_at, is_live):
    fetched = jnp.take(values, jnp.maximum(bucket_at, 0), axis=0)
    return jnp.where(is_live[:, None, None], fetched, jnp.zeros((), values.dtype))


def owner_work(q_in, g_in, k_in, v_in, keys, values, arrival, lengths, plen_live, group_size):
    softmax_scale = HD ** (-0.5)
    rows = q_in.shape[1]
    kv_local = keys.shape[1] // HD
    heads_per = q_in.shape[2] // (kv_local * HD)
    plen = keys.shape[0]
    per_block = max(1, min(group_size, 512 // (rows * kv_local * heads_per)))
    while group_size % per_block != 0:
        per_block = per_block - 1
    blocks = group_size // per_block
    tok_pos = jnp.arange(rows, dtype=jnp.int32)
    valid = tok_pos[None, :] < lengths[:, None]
    query = jnp.take(q_in, arrival, axis=0).reshape(
        blocks, per_block, rows, kv_local, heads_per, HD
    )
    grad_rows = jnp.take(g_in, arrival, axis=0)
    grads = jnp.where(valid[:, :, None], grad_rows, jnp.zeros((), grad_rows.dtype)).reshape(
        blocks, per_block, rows, kv_local, heads_per, HD
    )
    own_keys = jnp.take(k_in, arrival, axis=0).reshape(blocks, per_block, rows, kv_local, HD)
    own_values = jnp.take(v_in, arrival, axis=0).reshape(blocks, per_block, rows, kv_local, HD)
    pkeys = keys.reshape(plen, kv_local, HD)
    pvalues = values.reshape(plen, kv_local, HD)
    visible = (jnp.arange(plen, dtype=jnp.int32) < plen_live)[None, None, None, None, :]
    causal = (tok_pos[None, :] <= tok_pos[:, None])[None, :, None, None, :]
    f32 = jnp.float32

    def step(carry, inputs):
        acc_keys, acc_values = carry
        query_b, grads_b, okeys_b, ovalues_b = inputs
        prompt_scores = (
            jnp.einsum("ntkjd,pkd->ntkjp", query_b, pkeys, preferred_element_type=f32)
            * softmax_scale
        )
        local_scores = (
            jnp.einsum("ntkjd,nukd->ntkju", query_b, okeys_b, preferred_element_type=f32)
            * softmax_scale
        )
        row_max = jnp.maximum(
            jnp.max(jnp.where(visible, prompt_scores, -jnp.inf), axis=-1),
            jnp.max(jnp.where(causal, local_scores, -jnp.inf), axis=-1),
        )
        prompt_exp = jnp.where(visible, jnp.exp(prompt_scores - row_max[..., None]), 0.0)
        local_exp = jnp.where(causal, jnp.exp(local_scores - row_max[..., None]), 0.0)
        total = jnp.sum(prompt_exp, axis=-1) + jnp.sum(local_exp, axis=-1)
        prompt_probs = prompt_exp / total[..., None]
        local_probs = local_exp / total[..., None]
        prompt_dprobs = jnp.einsum("ntkjd,pkd->ntkjp", grads_b, pvalues, preferred_element_type=f32)
        local_dprobs = jnp.einsum(
            "ntkjd,nukd->ntkju", grads_b, ovalues_b, preferred_element_type=f32
        )
        delta = jnp.sum(prompt_probs * prompt_dprobs, axis=-1) + jnp.sum(
            local_probs * local_dprobs, axis=-1
        )
        prompt_ds = (prompt_probs * (prompt_dprobs - delta[..., None])).astype(jnp.bfloat16)
        local_ds = (local_probs * (local_dprobs - delta[..., None])).astype(jnp.bfloat16)
        prompt_half = prompt_probs.astype(jnp.bfloat16)
        local_half = local_probs.astype(jnp.bfloat16)
        grad_q = softmax_scale * (
            jnp.einsum("ntkjp,pkd->ntkjd", prompt_ds, pkeys, preferred_element_type=f32)
            + jnp.einsum("ntkju,nukd->ntkjd", local_ds, okeys_b, preferred_element_type=f32)
        )
        acc_keys = acc_keys + softmax_scale * jnp.einsum(
            "ntkjp,ntkjd->pkd", prompt_ds, query_b, preferred_element_type=f32
        )
        acc_values = acc_values + jnp.einsum(
            "ntkjp,ntkjd->pkd", prompt_half, grads_b, preferred_element_type=f32
        )
        grad_okeys = softmax_scale * jnp.einsum(
            "ntkju,ntkjd->nukd", local_ds, query_b, preferred_element_type=f32
        )
        grad_ovalues = jnp.einsum(
            "ntkju,ntkjd->nukd", local_half, grads_b, preferred_element_type=f32
        )
        return (
            (acc_keys, acc_values),
            (
                grad_q.astype(jnp.bfloat16),
                grad_okeys.astype(jnp.bfloat16),
                grad_ovalues.astype(jnp.bfloat16),
            ),
        )

    zeros_acc = jnp.zeros((plen, kv_local, HD), jnp.float32)
    (acc_keys, acc_values), (grad_q, grad_okeys, grad_ovalues) = lax.scan(
        step, (zeros_acc, zeros_acc), (query, grads, own_keys, own_values)
    )
    bucket_rows = q_in.shape[0]
    grad_q = grad_q.reshape(group_size, rows, q_in.shape[2])
    grad_okeys = grad_okeys.reshape(group_size, rows, k_in.shape[2])
    grad_ovalues = grad_ovalues.reshape(group_size, rows, k_in.shape[2])
    q_back = jnp.zeros((bucket_rows, rows, q_in.shape[2]), jnp.bfloat16).at[arrival].set(grad_q)
    k_back = jnp.zeros((bucket_rows, rows, k_in.shape[2]), jnp.bfloat16).at[arrival].set(grad_okeys)
    v_back = (
        jnp.zeros((bucket_rows, rows, k_in.shape[2]), jnp.bfloat16).at[arrival].set(grad_ovalues)
    )
    return (
        q_back,
        k_back,
        v_back,
        acc_keys.reshape(plen, -1).astype(jnp.bfloat16),
        acc_values.reshape(plen, -1).astype(jnp.bfloat16),
    )


def general(
    q_tokens,
    grad_tokens,
    roll_keys,
    roll_values,
    prompt_keys,
    prompt_values,
    slot_prompt,
    prompt_owner,
    roll_len,
    prompt_len,
):
    roll_count = lax.axis_size("roll")
    my_index = lax.axis_index("roll")
    slot_count = q_tokens.shape[0]
    bucket_cap = 2 * ((slot_count // 2 + roll_count - 1) // roll_count)
    bucket_at, is_live, source, filled = slot_tables(
        slot_prompt, prompt_owner, roll_count, slot_count, bucket_cap, my_index
    )
    arrival, lengths, plen_live = owner_tables(
        slot_prompt,
        prompt_owner,
        roll_len,
        prompt_len,
        roll_count,
        slot_count,
        bucket_cap,
        my_index,
        GROUP,
    )
    q_head, g_head, k_head, v_head = (
        lax.all_to_all(q_tokens, "kv", split_axis=2, concat_axis=1, tiled=True),
        lax.all_to_all(grad_tokens, "kv", split_axis=2, concat_axis=1, tiled=True),
        lax.all_to_all(roll_keys, "kv", split_axis=2, concat_axis=1, tiled=True),
        lax.all_to_all(roll_values, "kv", split_axis=2, concat_axis=1, tiled=True),
    )
    sent_q = pack_rows(q_head, source, filled)
    sent_g = pack_rows(g_head, source, filled)
    sent_k = pack_rows(k_head, source, filled)
    sent_v = pack_rows(v_head, source, filled)
    q_in, g_in, k_in, v_in = (
        lax.all_to_all(sent_q, "roll", split_axis=0, concat_axis=0, tiled=True),
        lax.all_to_all(sent_g, "roll", split_axis=0, concat_axis=0, tiled=True),
        lax.all_to_all(sent_k, "roll", split_axis=0, concat_axis=0, tiled=True),
        lax.all_to_all(sent_v, "roll", split_axis=0, concat_axis=0, tiled=True),
    )
    q_back, k_back, v_back, grad_pkeys, grad_pvalues = owner_work(
        q_in, g_in, k_in, v_in, prompt_keys, prompt_values, arrival, lengths, plen_live, GROUP
    )
    q_home, k_home, v_home = (
        lax.all_to_all(q_back, "roll", split_axis=0, concat_axis=0, tiled=True),
        lax.all_to_all(k_back, "roll", split_axis=0, concat_axis=0, tiled=True),
        lax.all_to_all(v_back, "roll", split_axis=0, concat_axis=0, tiled=True),
    )
    slot_q = unpack_rows(q_home, bucket_at, is_live)
    slot_k = unpack_rows(k_home, bucket_at, is_live)
    slot_v = unpack_rows(v_home, bucket_at, is_live)
    grad_query, grad_okeys, grad_ovalues = (
        lax.all_to_all(slot_q, "kv", split_axis=1, concat_axis=2, tiled=True),
        lax.all_to_all(slot_k, "kv", split_axis=1, concat_axis=2, tiled=True),
        lax.all_to_all(slot_v, "kv", split_axis=1, concat_axis=2, tiled=True),
    )
    return (grad_query, grad_okeys, grad_ovalues, grad_pkeys, grad_pvalues)


CAP = 8
N_KV = 8
N_ROLL = 32
SLOTS = 32
TSLOTS = 1024
RT = 24
PLEN = 2048
HG = 8
MESH = pl.DeviceIdType.MESH
BF = jnp.bfloat16
F32 = jnp.float32
LANES = GROUP * N_KV * HG // 2
KB = 512
OWN = RT * GROUP
OWN_UNIT = 6
LOG2E = 1.4426950408889634
VMEM_BYTES = 62 * 1024 * 1024


def dot(a, b):
    return jnp.dot(a, b, preferred_element_type=F32)


def dot_t(a, b):
    return lax.dot_general(a, b, (((1,), (1,)), ((), ())), preferred_element_type=F32)


def tables_kernel(where, owner, prompt_len, slots, lens, mats, mats_back, info):
    me, kv = where[0], where[1]
    x, y, c = me // 8, (me // 2) % 4, me % 2
    row = (1, TSLOTS)
    n = lax.broadcasted_iota(jnp.int32, row, 1)
    prompt = slots[...]
    live = prompt >= 0
    dest = jnp.zeros(row, jnp.int32)
    plen = jnp.int32(0)
    for p in range(N_ROLL):
        dest = jnp.where(prompt == p, owner[p], dest)
        plen = plen + jnp.where(owner[p] == me, prompt_len[p], 0)
    src = n // SLOTS
    xs, ys, cs = src // 8, (src // 2) % 4, src % 2
    xd, yd, cd = dest // 8, (dest // 2) % 4, dest % 2
    chip = xs * 4 + ys
    before = (
        lax.broadcasted_iota(jnp.int32, (128, 128), 0) < lax.broadcasted_iota(jnp.int32, (128, 128), 1)
    )
    both = jnp.concatenate(
        [jnp.where(before, 1.0, 0.0), jnp.ones((128, 128), F32)], axis=1
    ).astype(BF)

    def marks(at, count):
        rows = lax.broadcasted_iota(jnp.int32, (count, TSLOTS), 0)
        return jnp.where(rows == at, 1.0, 0.0)

    def rank_in(key, count):
        mark = marks(jnp.where(live, key, -1), count)
        total = jnp.zeros((count, 128), F32)
        parts = []
        for b in range(TSLOTS // 128):
            m = mark[:, b * 128 : (b + 1) * 128]
            o = dot(m.astype(BF), both)
            parts.append(jnp.sum(m * (o[:, :128] + total), axis=0, keepdims=True))
            total = total + o[:, 128:]
        return jnp.concatenate(parts, axis=1).astype(jnp.int32)

    first = (rank_in((chip * 2 + cd) * 4 + xd, 128), rank_in((chip * 2 + cd) * 4 + yd, 128))
    second = (
        rank_in(((xd * 4 + ys) * 2 + cd) * 4 + yd, 128),
        rank_in(((xs * 4 + yd) * 2 + cd) * 4 + xd, 128),
    )
    last = rank_in(dest, N_ROLL)
    most = jnp.maximum(jnp.maximum(first[0], first[1]), jnp.maximum(second[0], second[1]))
    info[0] = jnp.where(jnp.max(most) < CAP, 1, 0)
    info[1] = plen

    mine = live & (dest == me)
    near = live & (cd == c) & (chip == x * 4 + y)
    seat = n % SLOTS + jnp.where(cs == c, 0, SLOTS)
    seat = marks(jnp.where(near, seat, -1), 64).astype(BF)
    for h in (0, 1):
        s1, s2 = (xs, ys) if h == 0 else (ys, xs)
        d1, d2 = (xd, yd) if h == 0 else (yd, xd)
        mid = live & (cd == c) & ((ys == y) & (xd == x) if h == 0 else (xs == x) & (yd == y))

        def wide(place, rank, ok, part):
            return marks(jnp.where(ok, (place * 2 + part) * CAP + rank, -1), 64).astype(BF)

        mats[h, 0] = dot_t(marks(jnp.where(near, d1 * CAP + first[h], -1), 64).astype(BF), seat).astype(BF)
        turn = jnp.zeros((64, 64), F32)
        turn_back = jnp.zeros((64, 64), F32)
        ends = [jnp.zeros((64, 64), F32)] * 8
        end_back = jnp.zeros((64, 64), F32)
        for part in (0, 1):
            mats_back[h, part] = dot_t(seat, wide(d1, first[h], near, part)).astype(BF)
            a, b = wide(s1, first[h], mid, part), wide(d2, second[h], mid, part)
            turn = turn + dot_t(b, a)
            turn_back = turn_back + dot_t(a, b)
            a = wide(s2, second[h], mine, part)
            b = marks(jnp.where(mine, part * GROUP + last, -1), 64).astype(BF)
            end_back = end_back + dot_t(a, b)
            ends[3] = ends[3] + dot_t(b, a)
            if h == 0:
                continue
            tokens = [3 * kv, 3 * kv + 1, 3 * kv + 2, None] + [12 * part + 3 * i + 2 for i in range(4)]
            for t, token in enumerate(tokens):
                if token is not None:
                    valid = mine & (token < lens[...])
                    b = marks(jnp.where(valid, part * GROUP + last, -1), 64).astype(BF)
                    ends[t] = ends[t] + dot_t(b, a)
        mats[h, 1] = turn.astype(BF)
        for t in range(8):
            mats[h, 2 + t] = ends[t].astype(BF)
        mats_back[h, 2] = turn_back.astype(BF)
        mats_back[h, 3] = end_back.astype(BF)


def route_tables(slot_prompt, prompt_owner, roll_len, prompt_len):
    where = jnp.stack([lax.axis_index("roll"), lax.axis_index("kv")]).astype(jnp.int32)
    vm = pl.BlockSpec(memory_space=pltpu.VMEM)
    sm = pl.BlockSpec(memory_space=pltpu.SMEM)
    return pl.pallas_call(
        tables_kernel,
        out_shape=[
            jax.ShapeDtypeStruct((2, 10, 64, 64), BF),
            jax.ShapeDtypeStruct((2, 4, 64, 64), BF),
            jax.ShapeDtypeStruct((2,), jnp.int32),
        ],
        in_specs=[sm, sm, sm, vm, vm],
        out_specs=[vm, vm, sm],
        compiler_params=pltpu.CompilerParams(vmem_limit_bytes=VMEM_BYTES),
        name="tables",
    )(where, prompt_owner, prompt_len, slot_prompt.reshape(1, TSLOTS), roll_len.reshape(1, TSLOTS))


class Place:
    def __init__(self):
        self.kv = lax.axis_index("kv")
        self.me = lax.axis_index("roll")
        self.x = self.me // 8
        self.y = (self.me // 2) % 4
        self.c = self.me % 2

    def pos(self, axis):
        return self.x if axis == 0 else self.y

    def chip(self, axis, step):
        if axis == 0:
            return (self.kv, ((self.x + step) % 4) * 8 + self.y * 2 + self.c)
        return (self.kv, self.x * 8 + ((self.y + step) % 4) * 2 + self.c)

    def core(self):
        return (self.kv, self.x * 8 + self.y * 2 + 1 - self.c)

    def head(self, step):
        return ((self.kv + step) % N_KV, self.me)

    def greet(self):
        peers = [self.core()]
        peers += [self.chip(axis, i) for axis in (0, 1) for i in (1, 2, 3)]
        peers += [self.head(i) for i in range(1, N_KV)]
        barrier = pltpu.get_barrier_semaphore()
        for peer in peers:
            pl.semaphore_signal(barrier, inc=1, device_id=peer, device_id_type=MESH)
        pl.semaphore_wait(barrier, len(peers))


def remote(src, dst, send, recv, peer):
    return pltpu.make_async_remote_copy(
        src_ref=src, dst_ref=dst, send_sem=send, recv_sem=recv, device_id=peer, device_id_type=MESH
    )


def rows16(p):
    return pl.ds(pl.multiple_of(p * 16, 16), 16)


def axis_copies(place, axis, out, land, send, recv):
    p = place.pos(axis)
    return [
        remote(
            out.at[rows16((p + i) % 4)], land.at[rows16(p)], send.at[i - 1], recv.at[i - 1],
            place.chip(axis, i),
        )
        for i in (1, 2, 3)
    ]


def axis_send(place, axis, out, land, send, recv):
    for cp in axis_copies(place, axis, out, land, send, recv):
        cp.start()
    mine = rows16(place.pos(axis))
    land[mine, :] = out[mine, :]


def axis_wait(place, axis, out, land, send, recv):
    p = place.pos(axis)
    for i in (1, 2, 3):
        q = rows16((p - i + 4) % 4)
        remote(
            out.at[q], land.at[q], send.at[i - 1], recv.at[i - 1], place.chip(axis, i)
        ).wait_recv()


def head_copies(place, out, land, send, recv):
    return [
        remote(
            out.at[(place.kv + i) % N_KV], land.at[place.kv], send.at[i - 1], recv.at[i - 1],
            place.head(i),
        )
        for i in (4, 3, 5, 2, 6, 1, 7)
    ]


def head_send(place, out, land, send, recv):
    for cp in head_copies(place, out, land, send, recv):
        cp.start()
    land[place.kv] = out[place.kv]


def head_wait(place, out, land, send, recv):
    for i in range(1, N_KV):
        c = (place.kv - i + N_KV) % N_KV
        remote(
            out.at[c], land.at[c], send.at[i - 1], recv.at[i - 1], place.head(i)
        ).wait_recv()


def mega_kernel(
    info, q, g, k, v, mats, mats_back, keys_in, values_in,
    gq, gk, gv, dkeys, dvalues,
    oq, og, zk, zv, zq5, zg5, cq, cg, ck, cv, cq5, cg5, keys, values,
    s1a, s1b, r1a, r1b, s2a, s2b, r2a, r2b, s3, zu,
    qs, gs, ko, vo, kt, sc, dp, acck, accv, accok, accov, du, dsm, rzu, rzs,
    b1a, b1l, t1a, t1l, b2a, b2l, t2a, t2l, snda, sndl, rcva, rcvl,
    own_s, early_o, early_s, early_r, core_s, core_r, p1_s, p1_r, p2_s, p2_r, z_s, z_r,
    y_s, y_r, ys_s, ys_r, u1_s, u1_r, u2_s, u2_r, home_s, home_r,
):
    place = Place()
    scale = HD ** -0.5
    plen = info[1]

    def own_copies(t):
        names = [(q.at[t], oq.at[t], t, 0), (g.at[t], og.at[t], t, 1)]
        if t == 2:
            names += [(keys_in, keys, 3, 0), (values_in, values, 3, 1)]
        return [pltpu.make_async_copy(a, b, own_s.at[i, j]) for a, b, i, j in names]

    def core_copies(t):
        a, b, c, d = ((zk, ck, zv, cv), (zq5, cq5, zg5, cg5))[t - 3] if t > 2 else (
            q.at[t], cq.at[t], g.at[t], cg.at[t]
        )
        return [
            remote(a, b, core_s.at[t, 0], core_r.at[t, 0], place.core()),
            remote(c, d, core_s.at[t, 1], core_r.at[t, 1], place.core()),
        ]

    def lanes(at, size):
        return pl.ds(pl.multiple_of(at, size), size)

    def early(j, c, p):
        if j < 2:
            return (k, v)[j].at[:, :, lanes(c * HD, HD)], (zk, zv)[j].at[:, :, lanes(p * HD, HD)]
        src, dst = ((q, zq5), (g, zg5))[j - 2]
        return (
            src.at[2, :, lanes(c * 1024 + 512, 512)], dst.at[0, :, lanes(p * 512, 512)],
        )

    def early_copies(j):
        copies = []
        for i in (4, 3, 5, 2, 6, 1, 7):
            a, b = early(j, (place.kv + i) % N_KV, place.kv)
            copies.append(remote(a, b, early_s.at[j, i - 1], early_r.at[j, i - 1], place.head(i)))
        return copies

    def early_own(j):
        a, b = early(j, place.kv, place.kv)
        return pltpu.make_async_copy(a, b, early_o.at[j])

    def early_wait(j):
        for i in range(1, N_KV):
            c = (place.kv - i + N_KV) % N_KV
            a, b = early(j, c, c)
            remote(a, b, early_s.at[j, i - 1], early_r.at[j, i - 1], place.head(i)).wait_recv()
        early_own(j).wait()

    def part(first, rest, u, h):
        return first.at[h] if u == 2 else rest.at[u - (u > 2), h]

    def hop1(u, h):
        return (place, h, part(s1a, s1b, u, h), part(r1a, r1b, u, h), p1_s.at[u, h], p1_r.at[u, h])

    def hop2(u, h):
        return (
            place, 1 - h, part(s2a, s2b, u, h), part(r2a, r2b, u, h), p2_s.at[u, h], p2_r.at[u, h],
        )

    def hop3(u):
        return (place, s3.at[u], zu.at[u], z_s.at[u], z_r.at[u])

    def pack(u):
        t, f = u // 2, u % 2
        if f == 0:
            for cp in own_copies(t):
                cp.wait()
        arrived = core_copies(t) if f == 0 else []
        if u == 2:
            arrived += core_copies(3)
        if u == 5:
            arrived += core_copies(4)
        for cp in arrived:
            cp.wait_recv()
        for h in (0, 1):
            m = mats[h, 0, :32, :]
            dst = part(s1a, s1b, u, h)

            def put(a, b, tt, lo, hi, at):
                def one(o):
                    lanes = pl.ds(o, 512)
                    rows = jnp.concatenate([a[tt, :, lanes], b[tt, :, lanes]], axis=0)
                    return dot(m, rows).reshape(4, CAP, 512)

                both = jnp.concatenate([one(lo), one(hi)], axis=1).reshape(64, 512)
                dst[:, pl.ds(at, 512)] = both.astype(BF)

            big, bigo, small, smallo = (oq, cq, zk, ck) if h == 0 else (og, cg, zv, cv)
            for i in range(4):
                lo = i * 1024 + f * 512
                if u == 5:
                    put((zq5, zg5)[h], (cq5, cg5)[h], 0, i * 512, 2048 + i * 512, i * 512)
                else:
                    put(big, bigo, t, lo, lo + 4096, i * 512)
            if u == 2:
                for tt in range(3):
                    put(small, smallo, tt, 0, 512, 2048 + tt * 512)

    def send1(u):
        for h in (0, 1):
            axis_send(*hop1(u, h))

    def apply(m, src, dst):
        for o in range(0, src.shape[1], 512):
            dst[:, o : o + 512] = dot(m, src[:, o : o + 512]).astype(BF)

    def turn(u):
        for h in (0, 1):
            axis_wait(*hop1(u, h))
            apply(mats[h, 1], part(r1a, r1b, u, h), part(s2a, s2b, u, h))
            axis_send(*hop2(u, h))

    def finish(u):
        for h in (0, 1):
            axis_wait(*hop2(u, h))
            src = part(r2a, r2b, u, h)
            for i in range(4):
                m = 5 if h == 0 else 6 + i if u == 5 else 2 + u // 2
                o = dot(mats[h, m, :32, :], src[:, i * 512 : (i + 1) * 512]).astype(BF)
                dst = zu if u == 5 else s3
                dst[u, i, h] = o[:16]
                dst[u, i + 4, h] = o[16:]
            if u == 2:
                dst = (ko, vo)[h]
                for tt in range(3):
                    lo = 2048 + tt * 512
                    o = dot(mats[h, 5, :32, :], src[:, lo : lo + 512]).astype(BF)
                    for i in range(4):
                        at = tt * 128 + i * GROUP
                        dst[at : at + GROUP, :] = o[:16, i * HD : (i + 1) * HD]
                        dst[at + 64 : at + 64 + GROUP, :] = o[16:, i * HD : (i + 1) * HD]
        if u < 5:
            head_send(*hop3(u))

    def prepare(u):
        pl.when(u < 5)(lambda: head_wait(*hop3(u)))
        for h, dst in ((0, qs), (1, gs)):
            for j in range(HG // 2):
                dst[j * 128 : (j + 1) * 128, :] = zu[u, :, h, :, j * HD : (j + 1) * HD].reshape(128, HD)

    def fold_max(s):
        return jnp.max(s.reshape(s.shape[0] // 8, 8, LANES), axis=0)

    def fold_sum(s):
        return jnp.sum(s.reshape(s.shape[0] // 8, 8, LANES), axis=0)

    blocks = [slice(b * KB, (b + 1) * KB) for b in range(PLEN // KB)]
    tail = slice(PLEN, PLEN + OWN)

    def chunk(u):
        q_t = jnp.transpose(qs[...].astype(F32)).astype(BF)
        g_t = jnp.transpose(gs[...].astype(F32)).astype(BF)
        m8 = jnp.full((8, LANES), -jnp.inf, F32)
        for b, rows in enumerate(blocks):
            s = dot(keys[rows, :], q_t)
            if b > 0:
                seen = lax.broadcasted_iota(jnp.int32, (KB, 1), 0) + b * KB < plen
                s = jnp.where(seen, s, -jnp.inf)
            sc[rows, :] = s
            m8 = jnp.maximum(m8, fold_max(s))
        key = lax.broadcasted_iota(jnp.int32, (OWN, 1), 0)
        lane = lax.broadcasted_iota(jnp.int32, (1, LANES), 1)
        key_token = 3 * ((key % 128) // GROUP) + key // 128
        row_token = 3 * ((lane % 128) // GROUP) + u // 2
        same = (key % GROUP == lane % GROUP) & (key_token <= row_token)
        s = jnp.where(same, dot(ko[...], q_t), -jnp.inf)
        sc[tail, :] = s
        m8 = jnp.maximum(m8, fold_max(s))
        shift = jnp.max(m8, axis=0, keepdims=True) * (scale * LOG2E)

        l8 = jnp.zeros((8, LANES), F32)
        d8 = jnp.zeros((8, LANES), F32)
        for rows in blocks + [tail]:
            w = jnp.exp2(sc[rows, :] * (scale * LOG2E) - shift)
            d = dot(vo[...] if rows is tail else values[rows, :], g_t)
            sc[rows, :] = w
            dp[rows, :] = d
            l8 = l8 + fold_sum(w)
            d8 = d8 + fold_sum(w * d)
        inv = 1.0 / jnp.sum(l8, axis=0, keepdims=True)
        delta = jnp.sum(d8, axis=0, keepdims=True) * inv

        dq = jnp.zeros((HD, LANES), F32)
        for b, rows in enumerate([tail] + blocks):
            p = sc[rows, :] * inv
            ds = (p * (dp[rows, :] - delta)).astype(BF)
            p = p.astype(BF)
            if rows is tail:
                accov[...] += dot(p, gs[...])
                accok[...] += dot(ds, qs[...])
                k_t = jnp.transpose(ko[...].astype(F32)).astype(BF)
            else:
                accv[rows, :] += dot(p, gs[...])
                acck[rows, :] += dot(ds, qs[...])
                k_t = kt[b - 1]
            dq = dq + dot(k_t, ds)
            if rows is tail:
                pl.when(u == 4)(leave_own)
        dq = jnp.transpose(dq * scale).astype(BF)
        for j in range(HG // 2):
            du[u, :, :, j * HD : (j + 1) * HD] = dq[j * 128 : (j + 1) * 128, :].reshape(N_KV, GROUP, HD)

    def piece(rest, final, u, *at):
        return final.at[at] if u == OWN_UNIT else rest.at[(u, *at)]

    def back0(u):
        return (place, du.at[u], rzu.at[u], y_s.at[u], y_r.at[u])

    small0 = (place, dsm, rzs, ys_s, ys_r)

    def back1(u, h):
        return (
            place, 1 - h, piece(b1a, b1l, u, h), piece(t1a, t1l, u, h), u1_s.at[u, h], u1_r.at[u, h],
        )

    def back2(u, h):
        return (
            place, h, piece(b2a, b2l, u, h), piece(t2a, t2l, u, h), u2_s.at[u, h], u2_r.at[u, h],
        )

    def home(u, h):
        heads = pl.ds(4 * h, 4)
        return remote(
            piece(snda, sndl, u, heads), piece(rcva, rcvl, u, heads),
            home_s.at[u, h], home_r.at[u, h], place.core(),
        )

    def leave_own():
        for tt in range(3):
            at = slice(tt * 128, (tt + 1) * 128)
            dsm[:, :, at] = (accok[at, :] * scale).astype(BF).reshape(N_KV, GROUP, HD)
            dsm[:, :, 384 + tt * 128 : 512 + tt * 128] = accov[at, :].astype(BF).reshape(N_KV, GROUP, HD)
        head_send(*small0)

    def open_up(u):
        head_wait(*(small0 if u == OWN_UNIT else back0(u)))
        src = rzs if u == OWN_UNIT else rzu.at[u]
        wide = src.shape[-1]
        for h in (0, 1):
            m = mats_back[h, 3, :, :32]
            dst = piece(b1a, b1l, u, h)
            for lo in (0, 1):
                rows = jnp.concatenate([src[h * 4 + lo], src[h * 4 + 2 + lo]], axis=0)
                dst[:, lo * wide : (lo + 1) * wide] = dot(m, rows).astype(BF)
            axis_send(*back1(u, h))

    def turn_back(u):
        for h in (0, 1):
            axis_wait(*back1(u, h))
            apply(mats_back[h, 2], piece(t1a, t1l, u, h), piece(b2a, b2l, u, h))
            axis_send(*back2(u, h))

    def close(u):
        t, f = u // 2, u % 2
        for h in (0, 1):
            axis_wait(*back2(u, h))
            src = piece(t2a, t2l, u, h)
            wide = src.shape[-1] // 2
            for hh in (0, 1):
                m = mats_back[h, hh]
                for lo in (0, 1):
                    c = h * 4 + hh * 2 + lo
                    r = dot(m, src[:, lo * wide : (lo + 1) * wide]).astype(BF)
                    piece(snda, sndl, u, c)[...] = r[32:]
                    if u == OWN_UNIT:
                        lanes = slice(c * HD, (c + 1) * HD)
                        for tt in range(3):
                            gk[tt, :, lanes] = r[:32, tt * HD : (tt + 1) * HD]
                            gv[tt, :, lanes] = r[:32, 384 + tt * HD : 384 + (tt + 1) * HD]
                    else:
                        at = c * 1024 + f * 512
                        gq[t, :, at : at + 512] = r[:32]
            home(u, h).start()

    def settle(u):
        t, f = u // 2, u % 2
        for h in (0, 1):
            home(u, h).wait_recv()
        src = rcvl if u == OWN_UNIT else rcva.at[u]
        for c in range(N_KV):
            if u == OWN_UNIT:
                lanes = slice(c * HD, (c + 1) * HD)
                for tt in range(3):
                    at = tt * HD
                    gk[tt, :, lanes] = gk[tt, :, lanes] + src[c, :, at : at + HD]
                    gv[tt, :, lanes] = gv[tt, :, lanes] + src[c, :, at + 384 : at + 384 + HD]
            else:
                lanes = slice(c * 1024 + f * 512, c * 1024 + f * 512 + 512)
                gq[t, :, lanes] = gq[t, :, lanes] + src[c]

    def start(copies):
        for cp in copies:
            cp.start()

    for t in range(3):
        start(own_copies(t))
    place.greet()
    start(core_copies(0))
    for j in range(4):
        early_own(j).start()
        start(early_copies(j))
    pack(0)
    send1(0)
    start(core_copies(1))
    pack(1)
    turn(0)
    send1(1)
    early_wait(0)
    early_wait(1)
    start(core_copies(3))
    start(core_copies(2))
    finish(0)
    pack(2)
    send1(2)
    turn(1)
    pack(3)
    send1(3)
    early_wait(2)
    early_wait(3)
    start(core_copies(4))
    finish(1)
    turn(2)
    pack(4)
    send1(4)
    for b, rows in enumerate(blocks):
        kt[b] = jnp.transpose(keys[rows, :].astype(F32)).astype(BF)
    for ref in (acck, accv, accok, accov):
        ref[...] = jnp.zeros_like(ref)
    finish(2)
    turn(3)
    pack(5)
    send1(5)

    def body(i, _):
        late = i // 3
        u = (1 - late) * i + late * (3 + (i + 2) % 3)
        prepare(u)
        chunk(u)
        head_send(*back0(u))

        @pl.when(i == 0)
        def _():
            finish(3)
            turn(4)

        @pl.when(i == 1)
        def _():
            finish(4)
            turn(5)

        @pl.when(i == 2)
        def _():
            finish(5)
            open_up(0)

        @pl.when(i == 3)
        def _():
            open_up(1)
            turn_back(0)

        @pl.when(i == 4)
        def _():
            open_up(2)
            turn_back(1)
            close(0)
            open_up(5)

        return 0

    lax.fori_loop(0, 6, body, 0)
    turn_back(2)
    open_up(3)
    close(1)
    settle(0)
    turn_back(5)
    close(2)
    settle(1)
    for rows in blocks:
        dkeys[rows, :] = (acck[rows, :] * scale).astype(BF)
        dvalues[rows, :] = accv[rows, :].astype(BF)
    turn_back(3)
    open_up(OWN_UNIT)
    close(5)
    settle(2)
    open_up(4)
    turn_back(OWN_UNIT)
    close(3)
    settle(5)
    turn_back(4)
    close(OWN_UNIT)
    settle(3)
    close(4)
    settle(OWN_UNIT)
    settle(4)
    for t in range(5):
        for cp in core_copies(t):
            cp.wait_send()
    for j in range(4):
        for cp in early_copies(j):
            cp.wait_send()
    for cp in head_copies(*small0):
        cp.wait_send()
    for u in range(7):
        copies = []
        if u < 6:
            copies += head_copies(*back0(u))
        if u < 5:
            copies += head_copies(*hop3(u))
        for h in (0, 1):
            if u < 6:
                copies += axis_copies(*hop1(u, h)) + axis_copies(*hop2(u, h))
            copies += axis_copies(*back1(u, h)) + axis_copies(*back2(u, h)) + [home(u, h)]
        for cp in copies:
            cp.wait_send()


def mega(info, q, g, k, v, mats, mats_back, keys, values):
    vm = pl.BlockSpec(memory_space=pltpu.VMEM)
    sm = pl.BlockSpec(memory_space=pltpu.SMEM)
    hbm = pl.BlockSpec(memory_space=pl.ANY)
    sem = pltpu.SemaphoreType.DMA
    bf = lambda *shape: pltpu.VMEM(shape, BF)
    f32 = lambda *shape: pltpu.VMEM(shape, F32)
    rows = [
        bf(3, SLOTS, 8192), bf(3, SLOTS, 8192), bf(3, SLOTS, 1024), bf(3, SLOTS, 1024),
        bf(1, SLOTS, 4096), bf(1, SLOTS, 4096),
    ]
    there = [bf(2, 64, 3584), bf(5, 2, 64, 2048)]
    back = [bf(6, 2, 64, 1024), bf(2, 64, 1536)]
    home = [bf(6, N_KV, SLOTS, 512), bf(N_KV, SLOTS, 768)]
    hop_back = [sem((7, 2, 3)), sem((7, 2, 3))]
    hop = [sem((6, 2, 3)), sem((6, 2, 3))]
    head = [sem((6, 7)), sem((6, 7)), sem((7,)), sem((7,))]
    return pl.pallas_call(
        mega_kernel,
        out_shape=[
            jax.ShapeDtypeStruct((3, SLOTS, 8192), BF),
            jax.ShapeDtypeStruct((3, SLOTS, 1024), BF),
            jax.ShapeDtypeStruct((3, SLOTS, 1024), BF),
            jax.ShapeDtypeStruct((PLEN, HD), BF),
            jax.ShapeDtypeStruct((PLEN, HD), BF),
        ],
        in_specs=[sm] + [hbm] * 4 + [vm] * 2 + [hbm] * 2,
        out_specs=[vm] * 5,
        scratch_shapes=[
            *rows, *rows, bf(PLEN, HD), bf(PLEN, HD),
            *there, *there, *there, *there,
            bf(5, N_KV, 2, GROUP, 512), bf(6, N_KV, 2, GROUP, 512),
            bf(LANES, HD), bf(LANES, HD), bf(OWN, HD), bf(OWN, HD),
            bf(PLEN // KB, HD, KB),
            f32(PLEN + OWN, LANES), f32(PLEN + OWN, LANES),
            f32(PLEN, HD), f32(PLEN, HD), f32(OWN, HD), f32(OWN, HD),
            bf(6, N_KV, GROUP, 512), bf(N_KV, GROUP, 768),
            bf(6, N_KV, GROUP, 512), bf(N_KV, GROUP, 768),
            *back, *back, *back, *back, *home, *home,
            sem((4, 2)), sem((4,)), sem((4, 7)), sem((4, 7)), sem((5, 2)), sem((5, 2)), *hop, *hop,
            sem((5, 7)), sem((5, 7)), *head, *hop_back, *hop_back, sem((7, 2)), sem((7, 2)),
        ],
        compiler_params=pltpu.CompilerParams(
            collective_id=0, has_side_effects=True, vmem_limit_bytes=VMEM_BYTES
        ),
        name="mega",
    )(info, q, g, k, v, mats, mats_back, keys, values)


def settled_kernel(*refs):
    n = (len(refs) - 2) // 3
    ins, outs, held = refs[:n], refs[n : 2 * n], refs[2 * n : 3 * n]
    into, out_of = refs[-2], refs[-1]
    first = [pltpu.make_async_copy(ins[i], held[i], into.at[i]) for i in range(n)]
    then = [pltpu.make_async_copy(held[i], outs[i], out_of.at[i]) for i in range(n)]
    for cp in first:
        cp.start()
    for i in range(n):
        first[i].wait()
        then[i].start()
    for cp in then:
        cp.wait()


def settled(*arrays):
    hbm = pl.BlockSpec(memory_space=pl.ANY)
    return pl.pallas_call(
        settled_kernel,
        out_shape=[jax.ShapeDtypeStruct(a.shape, a.dtype) for a in arrays],
        in_specs=[hbm] * len(arrays),
        out_specs=[hbm] * len(arrays),
        scratch_shapes=[pltpu.VMEM(a.shape, a.dtype) for a in arrays]
        + [pltpu.SemaphoreType.DMA((len(arrays),))] * 2,
        compiler_params=pltpu.CompilerParams(vmem_limit_bytes=VMEM_BYTES),
        name="settled",
    )(*arrays)


def per_device(
    q_tokens, grad_tokens, roll_keys, roll_values, prompt_keys, prompt_values,
    slot_prompt, prompt_owner, roll_len, prompt_len,
):
    mats, mats_back, info = route_tables(slot_prompt, prompt_owner, roll_len, prompt_len)
    arrays = (q_tokens, grad_tokens, roll_keys, roll_values)

    def direct():
        tokens = (jnp.transpose(a, (1, 0, 2)) for a in arrays)
        gq, gk, gv, dkeys, dvalues = settled(
            *mega(info, *tokens, mats, mats_back, prompt_keys, prompt_values)
        )
        return (*(jnp.transpose(a, (1, 0, 2)) for a in (gq, gk, gv)), dkeys, dvalues)

    return lax.cond(
        info[0] > 0,
        direct,
        lambda: general(
            *arrays, prompt_keys, prompt_values, slot_prompt, prompt_owner, roll_len, prompt_len
        ),
    )


def solution(mesh):
    in_specs = (
        P("roll", "kv", None),
        P("roll", "kv", None),
        P("roll", "kv", None),
        P("roll", "kv", None),
        P("roll", "kv"),
        P("roll", "kv"),
        P(),
        P(),
        P(),
        P(),
    )
    out_specs = (
        P("roll", "kv", None),
        P("roll", "kv", None),
        P("roll", "kv", None),
        P("roll", "kv"),
        P("roll", "kv"),
    )
    return jax.shard_map(
        per_device, mesh=mesh, in_specs=in_specs, out_specs=out_specs, check_vma=False
    )
```
